128 devices in a mesh: batch: 2 (over x_lo), tensor: 8 (over z, core), grid: 8 (over x_hi, y).
Axes of the slice: x: 4 (x_hi: 2, x_lo: 2; x = x_hi * 2 + x_lo), y: 4, z: 4, core: 2. Of those that a mesh axis runs over, the one named last changes fastest.
Arguments:
- gate_pre: bfloat16 [2048, 27648], P(('batch', 'grid'), 'tensor'), may hold values from -6 to 6
- up_pre: bfloat16 [2048, 27648], P(('batch', 'grid'), 'tensor'), may hold values from -6 to 6
- out_grad: bfloat16 [2048, 5120], P(('batch', 'grid'), 'tensor'), may hold values from -0.59765625 to 0.59765625
- basis_in: bfloat16 [27648, 14336], P('tensor', ('batch', 'grid')), may hold values from -0.0390625 to 0.0390625
- basis_out: bfloat16 [5120, 5120], P('tensor'), may hold values from -0.078125 to 0.078125
- lengths: int32 [8], replicated, may hold values from 1 to 512, 2048 in all
Outputs:
- eigenvalues: float32 [5120, 14336], P('tensor', ('batch', 'grid'))
The draws below stay inside these ranges and needn't reach their ends.
Inputs may be any that keep to these rules, and one draw needn't show every extreme that they name: `lengths`: the 8 sequences are packed in order and fill all 2048 rows; the longest has exactly 512 tokens.
All inputs are finite; a program needn't handle non-finite values.
Results may differ from the reference program's by a relative error of at most 0.0039.
Values may be sent and summed in bfloat16 or wider, within the bound.
A program may use at most 128 MiB of HBM per device.

```python
import math
import jax
import jax.numpy as jnp
import numpy as np
from jax import lax

D = 5120
FF = 27648
KA = 14336
TOKENS = 2048
SEQS = 8
MAXLEN = 512


def shard_levels(key, dims, cuts, least, largest):
    loudness = 1.0
    for position, parts in cuts:
        heights = jax.random.uniform(jax.random.fold_in(jax.random.fold_in(key, 6), position), (parts,), jnp.float32, least / len(cuts), largest / len(cuts))
        loudness = loudness * jnp.repeat(jnp.exp(heights), dims[position] // parts).reshape((-1,) + (1,) * (len(dims) - 1 - position))
    return loudness


def split_up(count, total, limit, slope):
    weights = [(1 << 20) // math.isqrt(standing ** slope) + 1 for standing in range(2, count + 1)]
    spare, given = total - limit - (count - 1), [1] * (count - 1)
    while spare > 0:
        movable = [i for i in range(count - 1) if given[i] < limit]
        whole, budget = sum([weights[i] for i in movable]), spare
        for i in movable:
            addition = min(limit - given[i], max(1, budget * weights[i] // whole), spare)
            given[i] = given[i] + addition
            spare = spare - addition
    return np.array([limit] + given)


def uneven(own_key, count, total, bound, lean):
    if count == 2:
        one = jax.random.randint(own_key, (), max(1, total - bound), min(bound, total - 1) + 1)
        return jnp.stack([one, total - one])
    sizes = jnp.asarray(split_up(count, total, bound, lean), jnp.int32)
    pairs = (count - 1) // 2
    giver, taker = sizes[1:1 + 2 * pairs:2], sizes[2:2 + 2 * pairs:2]
    slack = jnp.minimum(giver - 1, bound - taker)
    passed = jax.random.randint(jax.random.fold_in(own_key, 1), (pairs,), 0, 1 << 20) % (slack + 1)
    sizes = sizes.at[1:1 + 2 * pairs:2].set(giver - passed).at[2:2 + 2 * pairs:2].set(taker + passed)
    return sizes[jax.random.permutation(jax.random.fold_in(own_key, 2), count)]


def scatter_about(stream_key, shape, spread, limit, shards=(), kind=jnp.bfloat16):
    array = jax.random.normal(stream_key, shape, jnp.float32) * spread
    if len(shards) > 0:
        array = shard_levels(stream_key, shape, shards, -0.22, 0.18) * array
    return jnp.clip(array, min=-limit, max=limit).astype(kind)


def setup_inputs(seed: int = 0) -> dict:
    streams_of = jax.random.split(jax.random.key(seed), 7)
    gate_pre = scatter_about(streams_of[0], (TOKENS, FF), 1.0, 6.0, ((0, 16), (1, 8)))
    up_pre = scatter_about(streams_of[1], (TOKENS, FF), 1.0, 6.0, ((0, 16), (1, 8)))
    out_grad = scatter_about(streams_of[2], (TOKENS, D), 0.1, 0.59765625, ((0, 16), (1, 8)))
    basis_in = scatter_about(streams_of[3], (FF, KA), FF ** -0.5, 0.0390625, ((0, 8), (1, 16)))
    basis_out = scatter_about(streams_of[4], (D, D), D ** -0.5, 0.078125, ((0, 8),))
    lengths = uneven(streams_of[5], SEQS, TOKENS, MAXLEN, 2).astype(jnp.int32)
    return {"gate_pre": gate_pre, "up_pre": up_pre, "out_grad": out_grad, "basis_in": basis_in, "basis_out": basis_out, "lengths": lengths}


def reference(gate_pre, up_pre, out_grad, basis_in, basis_out, lengths):
    activations = (jax.nn.silu(gate_pre.astype(jnp.float32)) * up_pre.astype(jnp.float32)).astype(jnp.bfloat16)
    rotated_in = jnp.dot(activations.astype(jnp.float32), basis_in.astype(jnp.float32), preferred_element_type=jnp.float32).astype(jnp.bfloat16)
    rotated_out = jnp.dot(out_grad.astype(jnp.float32), basis_out.astype(jnp.float32), preferred_element_type=jnp.float32).astype(jnp.bfloat16)
    offsets = (jnp.cumsum(lengths) - lengths).astype(jnp.int32)
    padded_in = jnp.concatenate([rotated_in, jnp.zeros((MAXLEN, KA), jnp.bfloat16)], 0)
    padded_out = jnp.concatenate([rotated_out, jnp.zeros((MAXLEN, D), jnp.bfloat16)], 0)

    def add_sequence(sequence, totals):
        begin_row = offsets[sequence].astype(jnp.int32)
        slab_in = lax.dynamic_slice_in_dim(padded_in, begin_row, MAXLEN, 0)
        row_keep = (jnp.arange(MAXLEN, dtype=jnp.int32) < lengths[sequence])[:, None]
        slab_in = jnp.where(row_keep, slab_in, jnp.zeros_like(slab_in))
        slab_out = lax.dynamic_slice_in_dim(padded_out, begin_row, MAXLEN, 0)
        product = jnp.dot(slab_out.T.astype(jnp.float32), slab_in.astype(jnp.float32), preferred_element_type=jnp.float32)
        return totals + product * product

    totals = lax.fori_loop(0, SEQS, add_sequence, jnp.zeros((D, KA), jnp.float32))
    return totals / SEQS
```

```python
import functools

import jax
import jax.numpy as jnp
from jax import lax
from jax.experimental import pallas as pl
from jax.experimental.pallas import tpu as pltpu
from jax.sharding import PartitionSpec as P

MESH = pl.DeviceIdType.MESH
BF = jnp.bfloat16
F32 = jnp.float32

TOK = 128
HALF = 64
QUART = 32
HID = 3456
COLS = 896
FEAT = 640
D = 5120
NT = 8
STEPS = 4
OWN = 8
PER = 6


def gather_kernel(
    gate_hbm, up_hbm, grad_hbm, bin_hbm, bout_hbm, r_hbm, gt_hbm,
    gate_v, up_v, grad_v, bin_v, bout_v,
    abuf, psend, precv, rbuf, gsend, grecv, gx, gy,
    load_sem, xy_send, xy_recv, rs_send, rs_recv, ag_send, ag_recv,
    gr_send, gr_recv, gg_send, gg_recv, out_sem,
):
    xl = lax.axis_index("batch")
    me = lax.axis_index("tensor")
    gi = lax.axis_index("grid")
    x = lax.div(gi, 4) * 2 + xl
    y = lax.rem(gi, 4)

    def at(dx, dy):
        xx = lax.rem(x + (dx + 4), 4)
        yy = lax.rem(y + (dy + 4), 4)
        return (lax.rem(xx, 2), me, lax.div(xx, 2) * 4 + yy)

    def block_of(dx, dy):
        b, _, g = at(dx, dy)
        return b * 8 + g

    def peer(k):
        return (xl, lax.rem(me + k, NT), gi)

    xp, xm, yp, ym = at(1, 0), at(-1, 0), at(0, 1), at(0, -1)

    loads = [
        pltpu.make_async_copy(s, d, load_sem.at[i])
        for i, (s, d) in enumerate(
            [(gate_hbm, gate_v), (up_hbm, up_v), (grad_hbm, grad_v), (bout_hbm, bout_v), (bin_hbm, bin_v)]
        )
    ]
    for c in loads:
        c.start()

    barrier = pltpu.get_barrier_semaphore()
    for dev in [xp, xm, yp, ym] + [peer(k) for k in range(1, NT)]:
        pl.semaphore_signal(barrier, inc=1, device_id=dev, device_id_type=MESH)
    pl.semaphore_wait(barrier, 4 + NT - 1)

    def remote(src, dst, ss, rs, dev):
        return pltpu.make_async_remote_copy(
            src_ref=src, dst_ref=dst, send_sem=ss, recv_sem=rs, device_id=dev, device_id_type=MESH
        )

    def piece(i, off=0, n=HALF):
        return abuf.at[pl.ds(pl.multiple_of(i * HALF + off, 16), n)]

    def xy(step, k):
        first = isinstance(step, int) and step < 0
        fwd = k % 4 >= 2
        minus = k % 2
        is_y = k >= 4
        if first:
            base = 4 if is_y else 0
            own, near, far = base, base + 1 + minus, base + 3
            dev = ((yp, ym) if is_y else (xp, xm))[minus]
        else:
            b = OWN + PER * step
            own = (4 if is_y else 0) + step
            near = b + (2 if is_y else 0) + minus
            far = b + 4 + (1 if is_y else 0)
            dev = ((xp, xm) if is_y else (yp, ym))[minus]
        if fwd:
            src, dst = piece(near, QUART * minus, QUART), piece(far, QUART * minus, QUART)
        else:
            src, dst = piece(own), piece(near)
        sem = k if first else 8 + 8 * step + k
        return remote(src, dst, xy_send.at[sem], xy_recv.at[sem], dev)

    def rs_copy(gran, row, m, k):
        there = lax.rem(me + k, NT)
        return remote(
            psend.at[pl.ds(pl.multiple_of(row + there * m, 16), m)],
            precv.at[k - 1, pl.ds(pl.multiple_of(lax.div(row, NT), 16), m)],
            rs_send.at[gran, k - 1], rs_recv.at[gran, k - 1], peer(k),
        )

    def ag_copy(gran, row, m, k):
        here = rbuf.at[pl.ds(pl.multiple_of(row + me * m, 16), m)]
        return remote(here, here, ag_send.at[gran, k - 1], ag_recv.at[gran, k - 1], peer(k))

    def ag_wait(gran, row, m, k):
        there = rbuf.at[pl.ds(pl.multiple_of(row + lax.rem(me + NT - k, NT) * m, 16), m)]
        remote(there, there, ag_send.at[gran, k - 1], ag_recv.at[gran, k - 1], peer(k)).wait_recv()

    def multiply(gran, row, n):
        rows = pl.ds(pl.multiple_of(row, 64), n)
        psend[rows, :] = jnp.dot(abuf[rows, :], bin_v[...], preferred_element_type=F32).astype(BF)
        for k in (4, 3, 5, 2, 6, 1, 7):
            rs_copy(gran, row, n // NT, k).start()

    def combine(gran, row, n):
        m = n // NT
        mine = pl.ds(pl.multiple_of(row + me * m, 16), m)
        total = psend[mine, :].astype(F32)
        for k in range(1, NT):
            rs_copy(gran, row, m, k).wait_recv()
            total = total + precv[k - 1, pl.ds(pl.multiple_of(lax.div(row, NT), 16), m), :].astype(F32)
        rbuf[mine, :] = total.astype(BF)
        for k in (4, 3, 5, 2, 6, 1, 7):
            ag_copy(gran, row, m, k).start()

    def store(i, block, half):
        return pltpu.make_async_copy(
            rbuf.at[pl.ds(pl.multiple_of(i * HALF, 64), HALF)],
            r_hbm.at[pl.ds(pl.multiple_of(block * TOK + half * HALF, 64), HALF)],
            out_sem.at[i],
        )

    def finish(gran, row, n):
        for k in range(1, NT):
            ag_wait(gran, row, n // NT, k)

    GH = FEAT // 2
    GQ = FEAT // 4

    def gg(phase, k):
        fwd = k % 4 >= 2
        minus = k % 2
        is_y = k >= 4
        buf = gy if is_y else gx
        if phase == 0:
            dev = ((yp, ym) if is_y else (xp, xm))[minus]
            if fwd:
                rows = pl.ds(GQ * minus, GQ)
                src, dst = buf.at[0, 1 + minus, rows], buf.at[0, 3, rows]
            else:
                src, dst = buf.at[0, 0], buf.at[0, 1 + minus]
        else:
            dev = ((xp, xm) if is_y else (yp, ym))[minus]
            if fwd:
                part = pl.ds(2 * minus, 2)
                src, dst = buf.at[1 + minus, part], buf.at[3, part]
            else:
                src, dst = buf.at[0], buf.at[1 + minus]
        sem = 8 * phase + k
        return remote(src, dst, gg_send.at[sem], gg_recv.at[sem], dev)

    def gr_copy(k):
        return remote(
            gsend.at[lax.rem(me + k, NT)], grecv.at[k - 1], gr_send.at[k - 1], gr_recv.at[k - 1], peer(k)
        )

    loads[0].wait()
    loads[1].wait()
    for half, i in ((0, 0), (1, 4)):
        g = gate_v[pl.ds(half * HALF, HALF), :].astype(F32)
        u = up_v[pl.ds(half * HALF, HALF), :].astype(F32)
        abuf[pl.ds(i * HALF, HALF), :] = (g / (1.0 + jnp.exp(-g)) * u).astype(BF)
        for k in (0, 1):
            xy(-1, 4 * half + k).start()

    loads[2].wait()
    loads[3].wait()

    def rotate(c, carry):
        cols = pl.ds(pl.multiple_of(c * FEAT, 128), FEAT)
        gsend[c] = jnp.dot(grad_v[...], bout_v[:, cols], preferred_element_type=F32).astype(BF)
        return carry

    lax.fori_loop(0, NT, rotate, 0)
    for k in (4, 3, 5, 2, 6, 1, 7):
        gr_copy(k).start()
    loads[4].wait()

    for k in (0, 1, 4, 5):
        xy(-1, k).wait_recv()
        xy(-1, k + 2).start()
    for k in (0, 1, 4, 5):
        xy(0, k).start()

    share = gsend[me].astype(F32)
    for k in range(1, NT):
        gr_copy(k).wait_recv()
        share = share + grecv[k - 1].astype(F32)
    share = share.T.astype(BF)
    gx[0, 0] = share[:GH]
    gy[0, 0] = share[GH:]
    for k in (0, 1, 4, 5):
        gg(0, k).start()

    for k in (2, 3, 6, 7):
        xy(-1, k).wait_recv()
    for k in (0, 1, 4, 5):
        xy(1, k).start()
    multiply(0, 0, 256)
    multiply(1, 256, 256)

    for k in (0, 1, 4, 5):
        gg(0, k).wait_recv()
        gg(0, k + 2).start()

    def step(j, carry):
        row = OWN * HALF + j * (PER * HALF)
        gran = 2 + 2 * j
        prev = jnp.where(j == 0, 0, row - PER * HALF)
        for k in (0, 1, 4, 5):
            xy(j, k).wait_recv()
            xy(j, k + 2).start()

        @pl.when(j < 2)
        def _():
            for k in (0, 1, 4, 5):
                xy(j + 2, k).start()

        @pl.when(j == 0)
        def _():
            for k in (2, 3, 6, 7):
                gg(0, k).wait_recv()
            for k in (0, 1, 4, 5):
                gg(1, k).start()

        @pl.when(j == 1)
        def _():
            for k in (0, 1, 4, 5):
                gg(1, k).wait_recv()
                gg(1, k + 2).start()

        multiply(gran, row, 256)

        @pl.when(j == 0)
        def _():
            combine(0, 0, 256)
            combine(1, 256, 256)

        @pl.when(j > 0)
        def _():
            combine(gran - 2, row - 384, 256)
            combine(gran - 1, row - 128, 128)

        for k in (2, 3, 6, 7):
            xy(j, k).wait_recv()
        multiply(gran + 1, row + 256, 128)
        return carry

    lax.fori_loop(0, STEPS, step, 0)
    last = OWN * HALF + (STEPS - 1) * PER * HALF
    combine(8, last, 256)
    combine(9, last + 256, 128)

    OFF = (0, -1, 1, 2)
    outs = []

    def put(c):
        c.start()
        outs.append(c)

    for k in (2, 3, 6, 7):
        gg(1, k).wait_recv()
    for a in range(4):
        for b in range(4):
            for buf, half, dx, dy in ((gx, 0, OFF[b], OFF[a]), (gy, 1, OFF[a], OFF[b])):
                put(
                    pltpu.make_async_copy(
                        buf.at[a, b],
                        gt_hbm.at[block_of(dx, dy), pl.ds(half * GH, GH)],
                        out_sem.at[32 + half * 16 + 4 * a + b],
                    )
                )
    for gran in range(2):
        finish(gran, 256 * gran, 256)
    for i in range(4):
        put(store(i, block_of(OFF[i], 0), 0))
        put(store(4 + i, block_of(0, OFF[i]), 1))
    for j in range(STEPS):
        row = OWN * HALF + j * PER * HALF
        b = OWN + PER * j
        finish(2 + 2 * j, row, 256)
        put(store(b, block_of(OFF[j], -1), 0))
        put(store(b + 1, block_of(OFF[j], 1), 0))
        put(store(b + 2, block_of(-1, OFF[j]), 1))
        put(store(b + 3, block_of(1, OFF[j]), 1))
        finish(3 + 2 * j, row + 256, 128)
        put(store(b + 4, block_of(OFF[j], 2), 0))
        put(store(b + 5, block_of(2, OFF[j]), 1))

    for k in range(8):
        xy(-1, k).wait_send()
        gg(0, k).wait_send()
        gg(1, k).wait_send()
    for j in range(STEPS):
        for k in range(8):
            xy(j, k).wait_send()
    for k in range(1, NT):
        gr_copy(k).wait_send()
        for gran in range(10):
            if gran < 2:
                row, n = 256 * gran, 256
            else:
                row, n = 512 + 384 * ((gran - 2) // 2) + 256 * (gran % 2), 128 if gran % 2 else 256
            rs_copy(gran, row, n // NT, k).wait_send()
            ag_copy(gran, row, n // NT, k).wait_send()
    for c in outs:
        c.wait()


def gather_call(gate, up, grad, basis_in, basis_out):
    vm = pltpu.VMEM
    dma = pltpu.SemaphoreType.DMA
    hbm = pl.BlockSpec(memory_space=pl.ANY)
    return pl.pallas_call(
        gather_kernel,
        out_shape=(
            jax.ShapeDtypeStruct((2048, COLS), BF),
            jax.ShapeDtypeStruct((16, FEAT, TOK), BF),
        ),
        in_specs=[hbm] * 5,
        out_specs=(hbm, hbm),
        scratch_shapes=[
            vm((TOK, HID), BF), vm((TOK, HID), BF), vm((TOK, FEAT), BF), vm((HID, COLS), BF), vm((FEAT, D), BF),
            vm((2048, HID), BF), vm((2048, COLS), BF), vm((NT - 1, 256, COLS), BF), vm((2048, COLS), BF),
            vm((NT, TOK, FEAT), BF), vm((NT - 1, TOK, FEAT), BF),
            vm((4, 4, FEAT // 2, TOK), BF), vm((4, 4, FEAT // 2, TOK), BF),
            dma((5,)), dma((40,)), dma((40,)), dma((10, 7)), dma((10, 7)), dma((10, 7)), dma((10, 7)),
            dma((7,)), dma((7,)), dma((16,)), dma((16,)), dma((64,)),
        ],
        compiler_params=pltpu.CompilerParams(
            collective_id=0, has_side_effects=True, vmem_limit_bytes=58 * 2**20
        ),
        name="rotate_gather",
    )(gate, up, grad, basis_in, basis_out)


KB = 256


def fit_kernel(lengths, r_ref, gt_ref, out_ref):
    out_ref[...] = jnp.zeros_like(out_ref)

    def add(s, begin):
        end = begin + lengths[s]
        first = lax.div(begin, KB)
        blocks = lax.div(end + KB - 1, KB) - first

        for n in (1, 2, 3):

            @pl.when(blocks == n)
            def _():
                row = pl.multiple_of(first * KB, KB)
                r = r_ref[pl.ds(row, n * KB), :]
                token = row + lax.broadcasted_iota(jnp.int32, r.shape, 0)
                r = jnp.where((token >= begin) & (token < end), r, jnp.zeros_like(r))
                g = jnp.concatenate([gt_ref[2 * first + i] for i in range(2 * n)], axis=1)
                p = jnp.dot(g, r, preferred_element_type=F32)
                out_ref[...] += p * p

        return end

    lax.fori_loop(0, 8, add, 0)
    out_ref[...] = out_ref[...] * 0.125


def fit_call(lengths, r, gt):
    whole = pl.BlockSpec(memory_space=pltpu.VMEM)
    return pl.pallas_call(
        fit_kernel,
        out_shape=jax.ShapeDtypeStruct((FEAT, COLS), F32),
        in_specs=[pl.BlockSpec(memory_space=pltpu.SMEM), whole, whole],
        out_specs=whole,
        compiler_params=pltpu.CompilerParams(vmem_limit_bytes=58 * 2**20),
        name="sequence_products",
    )(lengths, r, gt)


def shards(gate_pre, up_pre, out_grad, basis_in, basis_out, lengths):
    r, gt = gather_call(gate_pre, up_pre, out_grad, basis_in, basis_out)
    return fit_call(lengths, r, gt)


def solution(mesh):
    return jax.shard_map(
        shards,
        mesh=mesh,
        in_specs=(
            P(("batch", "grid"), "tensor"),
            P(("batch", "grid"), "tensor"),
            P(("batch", "grid"), "tensor"),
            P("tensor", ("batch", "grid")),
            P("tensor", None),
            P(),
        ),
        out_specs=P("tensor", ("batch", "grid")),
        check_vma=False,
    )
```

```python
import functools

import jax
import jax.numpy as jnp
from jax import lax
from jax.experimental import pallas as pl
from jax.experimental.pallas import tpu as pltpu
from jax.sharding import PartitionSpec as P

MESH = pl.DeviceIdType.MESH
BF = jnp.bfloat16
F32 = jnp.float32

TOK = 128
HALF = 64
QUART = 32
HID = 3456
COLS = 896
FEAT = 640
D = 5120
NT = 8
STEPS = 4
OWN = 8
PER = 6


def gather_kernel(
    gate_hbm, up_hbm, grad_hbm, bin_hbm, bout_hbm, r_hbm, gt_hbm,
    gate_v, up_v, grad_v, bin_v, bout_v,
    abuf, pbuf, crecv, zsend, zrecv, rbuf, gpart, gcrecv, gzsend, gzrecv, gx, gy,
    load_sem, xy_send, xy_recv, ce_send, ce_recv, rs_send, rs_recv, ag_send, ag_recv, cf_send, cf_recv,
    gr_send, gr_recv, gg_send, gg_recv, out_sem,
):
    xl = lax.axis_index("batch")
    me = lax.axis_index("tensor")
    gi = lax.axis_index("grid")
    x = lax.div(gi, 4) * 2 + xl
    y = lax.rem(gi, 4)
    z = lax.div(me, 2)
    core = lax.rem(me, 2)

    def at(dx, dy):
        xx = lax.rem(x + (dx + 4), 4)
        yy = lax.rem(y + (dy + 4), 4)
        return (lax.rem(xx, 2), me, lax.div(xx, 2) * 4 + yy)

    def block_of(dx, dy):
        b, _, g = at(dx, dy)
        return b * 8 + g

    def zpeer(k):
        return (xl, lax.rem(z + k, 4) * 2 + core, gi)

    partner = (xl, z * 2 + 1 - core, gi)
    xp, xm, yp, ym = at(1, 0), at(-1, 0), at(0, 1), at(0, -1)

    loads = [
        pltpu.make_async_copy(s, d, load_sem.at[i])
        for i, (s, d) in enumerate(
            [(gate_hbm, gate_v), (up_hbm, up_v), (grad_hbm, grad_v), (bout_hbm, bout_v), (bin_hbm, bin_v)]
        )
    ]
    for c in loads:
        c.start()

    barrier = pltpu.get_barrier_semaphore()
    for dev in [xp, xm, yp, ym, partner, zpeer(1), zpeer(2), zpeer(3)]:
        pl.semaphore_signal(barrier, inc=1, device_id=dev, device_id_type=MESH)
    pl.semaphore_wait(barrier, 8)

    def remote(src, dst, ss, rs, dev):
        return pltpu.make_async_remote_copy(
            src_ref=src, dst_ref=dst, send_sem=ss, recv_sem=rs, device_id=dev, device_id_type=MESH
        )

    def rows_at(i, n):
        return pl.ds(pl.multiple_of(i, 16), n)

    def piece(i, off=0, n=HALF):
        return abuf.at[rows_at(i * HALF + off, n)]

    def xy(step, k):
        first = isinstance(step, int) and step < 0
        fwd = k % 4 >= 2
        minus = k % 2
        is_y = k >= 4
        if first:
            base = 4 if is_y else 0
            own, near, far = base, base + 1 + minus, base + 3
            dev = ((yp, ym) if is_y else (xp, xm))[minus]
        else:
            b = OWN + PER * step
            own = (4 if is_y else 0) + step
            near = b + (2 if is_y else 0) + minus
            far = b + 4 + (1 if is_y else 0)
            dev = ((xp, xm) if is_y else (yp, ym))[minus]
        if fwd:
            src, dst = piece(near, QUART * minus, QUART), piece(far, QUART * minus, QUART)
        else:
            src, dst = piece(own), piece(near)
        sem = k if first else 8 + 8 * step + k
        return remote(src, dst, xy_send.at[sem], xy_recv.at[sem], dev)

    def swap(gran, row, n):
        h = n // 2
        return remote(
            pbuf.at[rows_at(row + (1 - core) * h, h)], crecv.at[rows_at(lax.div(row, 2), h)],
            ce_send.at[gran], ce_recv.at[gran], partner,
        )

    def rs_copy(gran, row, n, k):
        m = n // 8
        return remote(
            zsend.at[rows_at(lax.div(row, 2) + lax.rem(z + k, 4) * m, m)],
            zrecv.at[k - 1, rows_at(lax.div(row, 8), m)],
            rs_send.at[gran, k - 1], rs_recv.at[gran, k - 1], zpeer(k),
        )

    def ag_copy(gran, row, n, k):
        m = n // 8
        here = rbuf.at[rows_at(row + core * (n // 2) + z * m, m)]
        return remote(here, here, ag_send.at[gran, k - 1], ag_recv.at[gran, k - 1], zpeer(k))

    def ag_arrival(gran, row, n, k):
        m = n // 8
        there = rbuf.at[rows_at(row + core * (n // 2) + lax.rem(z + 4 - k, 4) * m, m)]
        return remote(there, there, ag_send.at[gran, k - 1], ag_recv.at[gran, k - 1], zpeer(k))

    def half_copy(gran, row, n, c):
        there = rbuf.at[rows_at(row + c * (n // 2), n // 2)]
        return remote(there, there, cf_send.at[gran], cf_recv.at[gran], partner)

    def multiply(gran, row, n):
        rows = rows_at(row, n)
        pbuf[rows, :] = jnp.dot(abuf[rows, :], bin_v[...], preferred_element_type=F32).astype(BF)
        swap(gran, row, n).start()

    def pair(gran, row, n):
        h = n // 2
        swap(gran, row, n).wait_recv()
        mine = pbuf[rows_at(row + core * h, h), :].astype(F32)
        theirs = crecv[rows_at(lax.div(row, 2), h), :].astype(F32)
        zsend[rows_at(lax.div(row, 2), h), :] = (mine + theirs).astype(BF)
        for k in (2, 1, 3):
            rs_copy(gran, row, n, k).start()

    def combine(gran, row, n):
        h, m = n // 2, n // 8
        total = pbuf[rows_at(row + core * h + z * m, m), :].astype(F32)
        total = total + crecv[rows_at(lax.div(row, 2) + z * m, m), :].astype(F32)
        for k in (1, 3, 2):
            rs_copy(gran, row, n, k).wait_recv()
            total = total + zrecv[k - 1, rows_at(lax.div(row, 8), m), :].astype(F32)
        rbuf[rows_at(row + core * h + z * m, m), :] = total.astype(BF)
        for k in (2, 1, 3):
            ag_copy(gran, row, n, k).start()

    def spread(gran, row, n):
        for k in (1, 3, 2):
            ag_arrival(gran, row, n, k).wait_recv()
        half_copy(gran, row, n, core).start()

    def finish(gran, row, n):
        half_copy(gran, row, n, 1 - core).wait_recv()

    def store(i, block, half):
        return pltpu.make_async_copy(
            rbuf.at[rows_at(i * HALF, HALF)],
            r_hbm.at[rows_at(block * TOK + half * HALF, HALF)],
            out_sem.at[i],
        )

    GH = FEAT // 2
    GQ = FEAT // 4

    def gg(phase, k):
        fwd = k % 4 >= 2
        minus = k % 2
        is_y = k >= 4
        buf = gy if is_y else gx
        if phase == 0:
            dev = ((yp, ym) if is_y else (xp, xm))[minus]
            if fwd:
                rows = pl.ds(GQ * minus, GQ)
                src, dst = buf.at[0, 1 + minus, rows], buf.at[0, 3, rows]
            else:
                src, dst = buf.at[0, 0], buf.at[0, 1 + minus]
        else:
            dev = ((xp, xm) if is_y else (yp, ym))[minus]
            if fwd:
                part = pl.ds(2 * minus, 2)
                src, dst = buf.at[1 + minus, part], buf.at[3, part]
            else:
                src, dst = buf.at[0], buf.at[1 + minus]
        sem = 8 * phase + k
        return remote(src, dst, gg_send.at[sem], gg_recv.at[sem], dev)

    def gr_swap():
        return remote(gpart.at[1 - core], gcrecv, gr_send.at[0], gr_recv.at[0], partner)

    def gr_copy(k):
        return remote(gzsend.at[lax.rem(z + k, 4)], gzrecv.at[k - 1], gr_send.at[k], gr_recv.at[k], zpeer(k))

    loads[0].wait()
    loads[1].wait()
    for half, i in ((0, 0), (1, 4)):
        g = gate_v[pl.ds(half * HALF, HALF), :].astype(F32)
        u = up_v[pl.ds(half * HALF, HALF), :].astype(F32)
        abuf[pl.ds(i * HALF, HALF), :] = (g / (1.0 + jnp.exp(-g)) * u).astype(BF)
        for k in (0, 1):
            xy(-1, 4 * half + k).start()

    loads[2].wait()
    loads[3].wait()

    def rotate(c, carry):
        cols = pl.ds(pl.multiple_of(c * FEAT, 128), FEAT)
        gpart[lax.rem(c, 2), lax.div(c, 2)] = jnp.dot(grad_v[...], bout_v[:, cols], preferred_element_type=F32)
        return carry

    lax.fori_loop(0, NT, rotate, 0)
    gr_swap().start()
    gr_swap().wait_recv()
    for k in (2, 1, 3):
        there = lax.rem(z + k, 4)
        gzsend[there] = (gpart[core, there] + gcrecv[there]).astype(BF)
        gr_copy(k).start()
    loads[4].wait()

    for k in (0, 1, 4, 5):
        xy(-1, k).wait_recv()
        xy(-1, k + 2).start()
    for k in (0, 1, 4, 5):
        xy(0, k).start()

    share = gpart[core, z] + gcrecv[z]
    for k in (1, 3, 2):
        gr_copy(k).wait_recv()
        share = share + gzrecv[k - 1].astype(F32)
    share = share.T.astype(BF)
    gx[0, 0] = share[:GH]
    gy[0, 0] = share[GH:]

    for k in (2, 3, 6, 7):
        xy(-1, k).wait_recv()
    for k in (0, 1, 4, 5):
        xy(1, k).start()

    def own(stage):
        lax.fori_loop(0, 2, lambda g, c: (stage(g, g * 256, 256), c)[1], 0)

    own(multiply)
    own(pair)
    own(combine)

    def step(j, carry):
        row = OWN * HALF + j * (PER * HALF)
        near = (2 + 2 * j, row, 256)
        far = (3 + 2 * j, row + 256, 128)
        old = (1 + 2 * j, row - 128, 128)
        later = pl.when(j > 0)
        for k in (0, 1, 4, 5):
            xy(j, k).wait_recv()
            xy(j, k + 2).start()

        @pl.when(j < 2)
        def _():
            for k in (0, 1, 4, 5):
                xy(j + 2, k).start()

        @pl.when(j == 0)
        def _():
            for k in (0, 1, 4, 5):
                gg(0, k).start()

        @pl.when(j == 1)
        def _():
            for k in (0, 1, 4, 5):
                gg(0, k).wait_recv()
                gg(0, k + 2).start()

        @pl.when(j == 3)
        def _():
            for k in (2, 3, 6, 7):
                gg(0, k).wait_recv()
            for k in (0, 1, 4, 5):
                gg(1, k).start()

        multiply(*near)

        @pl.when(j == 0)
        def _():
            own(spread)

        @later
        def _():
            combine(*old)

        pair(*near)

        @later
        def _():
            spread(*old)

        combine(*near)
        for k in (2, 3, 6, 7):
            xy(j, k).wait_recv()
        multiply(*far)
        spread(*near)
        pair(*far)
        return carry

    lax.fori_loop(0, STEPS, step, 0)
    last = (9, 2048 - 128, 128)
    combine(*last)

    OFF = (0, -1, 1, 2)
    outs = []

    def put(c):
        c.start()
        outs.append(c)

    def granules():
        for g in range(10):
            yield (g, 256 * g, 256) if g < 2 else (g, 512 + 384 * ((g - 2) // 2) + 256 * (g % 2), 128 if g % 2 else 256)

    every = list(granules())
    for g in every[:9]:
        finish(*g)
    for i in range(4):
        put(store(i, block_of(OFF[i], 0), 0))
        put(store(4 + i, block_of(0, OFF[i]), 1))
    for j in range(STEPS):
        b = OWN + PER * j
        put(store(b, block_of(OFF[j], -1), 0))
        put(store(b + 1, block_of(OFF[j], 1), 0))
        put(store(b + 2, block_of(-1, OFF[j]), 1))
        put(store(b + 3, block_of(1, OFF[j]), 1))
        if j < 3:
            put(store(b + 4, block_of(OFF[j], 2), 0))
            put(store(b + 5, block_of(2, OFF[j]), 1))
    spread(*last)
    for k in (0, 1, 4, 5):
        gg(1, k).wait_recv()
        gg(1, k + 2).start()

    def put_gradient(a):
        for b in range(4):
            for buf, half, dx, dy in ((gx, 0, OFF[b], OFF[a]), (gy, 1, OFF[a], OFF[b])):
                put(
                    pltpu.make_async_copy(
                        buf.at[a, b],
                        gt_hbm.at[block_of(dx, dy), pl.ds(half * GH, GH)],
                        out_sem.at[32 + half * 16 + 4 * a + b],
                    )
                )

    for a in range(3):
        put_gradient(a)
    finish(*last)
    put(store(30, block_of(2, 2), 0))
    put(store(31, block_of(2, 2), 1))

    for k in range(8):
        xy(-1, k).wait_send()
        gg(0, k).wait_send()
    for j in range(STEPS):
        for k in range(8):
            xy(j, k).wait_send()
    gr_swap().wait_send()
    for k in (1, 2, 3):
        gr_copy(k).wait_send()
    for g in every:
        swap(*g).wait_send()
        half_copy(*g, core).wait_send()
        for k in (1, 2, 3):
            rs_copy(*g, k).wait_send()
            ag_copy(*g, k).wait_send()
    for k in (2, 3, 6, 7):
        gg(1, k).wait_recv()
    put_gradient(3)
    for k in range(8):
        gg(1, k).wait_send()
    for c in outs:
        c.wait()


def gather_call(gate, up, grad, basis_in, basis_out):
    vm = pltpu.VMEM
    dma = pltpu.SemaphoreType.DMA
    hbm = pl.BlockSpec(memory_space=pl.ANY)
    return pl.pallas_call(
        gather_kernel,
        out_shape=(
            jax.ShapeDtypeStruct((2048, COLS), BF),
            jax.ShapeDtypeStruct((16, FEAT, TOK), BF),
        ),
        in_specs=[hbm] * 5,
        out_specs=(hbm, hbm),
        scratch_shapes=[
            vm((TOK, HID), BF), vm((TOK, HID), BF), vm((TOK, FEAT), BF), vm((HID, COLS), BF), vm((FEAT, D), BF),
            vm((2048, HID), BF), vm((2048, COLS), BF), vm((1024, COLS), BF), vm((1024, COLS), BF),
            vm((3, 256, COLS), BF), vm((2048, COLS), BF),
            vm((2, 4, TOK, FEAT), F32), vm((4, TOK, FEAT), F32), vm((4, TOK, FEAT), BF), vm((3, TOK, FEAT), BF),
            vm((4, 4, FEAT // 2, TOK), BF), vm((4, 4, FEAT // 2, TOK), BF),
            dma((5,)), dma((40,)), dma((40,)), dma((10,)), dma((10,)), dma((10, 3)), dma((10, 3)),
            dma((10, 3)), dma((10, 3)), dma((10,)), dma((10,)),
            dma((4,)), dma((4,)), dma((16,)), dma((16,)), dma((64,)),
        ],
        compiler_params=pltpu.CompilerParams(
            collective_id=0, has_side_effects=True, vmem_limit_bytes=58 * 2**20
        ),
        name="rotate_gather",
    )(gate, up, grad, basis_in, basis_out)


KB = 256


def fit_kernel(lengths, r_ref, gt_ref, out_ref):
    out_ref[...] = jnp.zeros_like(out_ref)

    def add(s, begin):
        end = begin + lengths[s]
        first = lax.div(begin, KB)
        blocks = lax.div(end + KB - 1, KB) - first

        for n in (1, 2, 3):

            @pl.when(blocks == n)
            def _():
                row = pl.multiple_of(first * KB, KB)
                r = r_ref[pl.ds(row, n * KB), :]
                token = row + lax.broadcasted_iota(jnp.int32, r.shape, 0)
                r = jnp.where((token >= begin) & (token < end), r, jnp.zeros_like(r))
                g = jnp.concatenate([gt_ref[2 * first + i] for i in range(2 * n)], axis=1)
                p = jnp.dot(g, r, preferred_element_type=F32)
                out_ref[...] += p * p

        return end

    lax.fori_loop(0, 8, add, 0)
    out_ref[...] = out_ref[...] * 0.125


def fit_call(lengths, r, gt):
    whole = pl.BlockSpec(memory_space=pltpu.VMEM)
    return pl.pallas_call(
        fit_kernel,
        out_shape=jax.ShapeDtypeStruct((FEAT, COLS), F32),
        in_specs=[pl.BlockSpec(memory_space=pltpu.SMEM), whole, whole],
        out_specs=whole,
        compiler_params=pltpu.CompilerParams(vmem_limit_bytes=58 * 2**20),
        name="sequence_products",
    )(lengths, r, gt)


def shards(gate_pre, up_pre, out_grad, basis_in, basis_out, lengths):
    r, gt = gather_call(gate_pre, up_pre, out_grad, basis_in, basis_out)
    return fit_call(lengths, r, gt)


def solution(mesh):
    return jax.shard_map(
        shards,
        mesh=mesh,
        in_specs=(
            P(("batch", "grid"), "tensor"),
            P(("batch", "grid"), "tensor"),
            P(("batch", "grid"), "tensor"),
            P("tensor", ("batch", "grid")),
            P("tensor", None),
            P(),
        ),
        out_specs=P("tensor", ("batch", "grid")),
        check_vma=False,
    )
```

```python
import functools

import jax
import jax.numpy as jnp
from jax import lax
from jax.experimental import pallas as pl
from jax.experimental.pallas import tpu as pltpu
from jax.sharding import PartitionSpec as P

MESH = pl.DeviceIdType.MESH
BF = jnp.bfloat16
F32 = jnp.float32

TOK = 128
HALF = 64
QUART = 32
HID = 3456
COLS = 896
FEAT = 640
D = 5120
NT = 8
STEPS = 4
OWN = 8
PER = 6


def gather_kernel(
    gate_hbm, up_hbm, grad_hbm, bin_hbm, bout_hbm, r_hbm, gt_hbm,
    gate_v, up_v, grad_v, bin_v, bout_v,
    abuf, pbuf, crecv, zsend, zrecv, rbuf, gpart, gcrecv, gzrecv, gx, gy,
    load_sem, xy_send, xy_recv, ce_send, ce_recv, rs_send, rs_recv, ag_send, ag_recv, cf_send, cf_recv,
    gr_send, gr_recv, gg_send, gg_recv, out_sem,
):
    xl = lax.axis_index("batch")
    me = lax.axis_index("tensor")
    gi = lax.axis_index("grid")
    x = lax.div(gi, 4) * 2 + xl
    y = lax.rem(gi, 4)
    z = lax.div(me, 2)
    core = lax.rem(me, 2)

    def at(dx, dy):
        xx = lax.rem(x + (dx + 4), 4)
        yy = lax.rem(y + (dy + 4), 4)
        return (lax.rem(xx, 2), me, lax.div(xx, 2) * 4 + yy)

    def block_of(dx, dy):
        b, _, g = at(dx, dy)
        return b * 8 + g

    def zpeer(k):
        return (xl, lax.rem(z + k, 4) * 2 + core, gi)

    partner = (xl, z * 2 + 1 - core, gi)
    xp, xm, yp, ym = at(1, 0), at(-1, 0), at(0, 1), at(0, -1)

    loads = [
        pltpu.make_async_copy(s, d, load_sem.at[i])
        for i, (s, d) in enumerate(
            [(gate_hbm, gate_v), (up_hbm, up_v), (grad_hbm, grad_v), (bout_hbm, bout_v), (bin_hbm, bin_v)]
        )
    ]
    loads[0].start()
    loads[1].start()

    barrier = pltpu.get_barrier_semaphore()
    for dev in [xp, xm, yp, ym, partner, zpeer(1), zpeer(2), zpeer(3)]:
        pl.semaphore_signal(barrier, inc=1, device_id=dev, device_id_type=MESH)
    pl.semaphore_wait(barrier, 8)

    def remote(src, dst, ss, rs, dev):
        return pltpu.make_async_remote_copy(
            src_ref=src, dst_ref=dst, send_sem=ss, recv_sem=rs, device_id=dev, device_id_type=MESH
        )

    def rows_at(i, n):
        return pl.ds(pl.multiple_of(i, 16), n)

    def piece(i, off=0, n=HALF):
        return abuf.at[rows_at(i * HALF + off, n)]

    def xy(step, k):
        first = isinstance(step, int) and step < 0
        fwd = k % 4 >= 2
        minus = k % 2
        is_y = k >= 4
        if first:
            base = 4 if is_y else 0
            own, near, far = base, base + 1 + minus, base + 3
            dev = ((yp, ym) if is_y else (xp, xm))[minus]
        else:
            b = OWN + PER * step
            own = (4 if is_y else 0) + step
            near = b + (2 if is_y else 0) + minus
            far = b + 4 + (1 if is_y else 0)
            dev = ((xp, xm) if is_y else (yp, ym))[minus]
        if fwd:
            src, dst = piece(near, QUART * minus, QUART), piece(far, QUART * minus, QUART)
        else:
            src, dst = piece(own), piece(near)
        sem = k if first else 8 + 8 * step + k
        return remote(src, dst, xy_send.at[sem], xy_recv.at[sem], dev)

    def swap(gran, row, n):
        h = n // 2
        return remote(
            pbuf.at[rows_at(row + (1 - core) * h, h)], crecv.at[rows_at(lax.div(row, 2), h)],
            ce_send.at[gran], ce_recv.at[gran], partner,
        )

    def rs_copy(gran, row, n, k):
        m = n // 8
        return remote(
            zsend.at[rows_at(lax.div(row, 2) + lax.rem(z + k, 4) * m, m)],
            zrecv.at[k - 1, rows_at(lax.div(row, 8), m)],
            rs_send.at[gran, k - 1], rs_recv.at[gran, k - 1], zpeer(k),
        )

    def ag_copy(gran, row, n, k):
        m = n // 8
        here = rbuf.at[rows_at(row + core * (n // 2) + z * m, m)]
        return remote(here, here, ag_send.at[gran, k - 1], ag_recv.at[gran, k - 1], zpeer(k))

    def ag_arrival(gran, row, n, k):
        m = n // 8
        there = rbuf.at[rows_at(row + core * (n // 2) + lax.rem(z + 4 - k, 4) * m, m)]
        return remote(there, there, ag_send.at[gran, k - 1], ag_recv.at[gran, k - 1], zpeer(k))

    def half_copy(gran, row, n, c):
        there = rbuf.at[rows_at(row + c * (n // 2), n // 2)]
        return remote(there, there, cf_send.at[gran], cf_recv.at[gran], partner)

    def multiply(gran, row, n):
        rows = rows_at(row, n)
        pbuf[rows, :] = jnp.dot(abuf[rows, :], bin_v[...], preferred_element_type=F32)
        swap(gran, row, n).start()

    def pair(gran, row, n):
        h = n // 2
        swap(gran, row, n).wait_recv()
        mine = pbuf[rows_at(row + core * h, h), :]
        theirs = crecv[rows_at(lax.div(row, 2), h), :]
        zsend[rows_at(lax.div(row, 2), h), :] = (mine + theirs).astype(BF)
        for k in (2, 1, 3):
            rs_copy(gran, row, n, k).start()

    def combine(gran, row, n):
        h, m = n // 2, n // 8
        total = pbuf[rows_at(row + core * h + z * m, m), :] + crecv[rows_at(lax.div(row, 2) + z * m, m), :]
        for k in (1, 3, 2):
            rs_copy(gran, row, n, k).wait_recv()
            total = total + zrecv[k - 1, rows_at(lax.div(row, 8), m), :].astype(F32)
        rbuf[rows_at(row + core * h + z * m, m), :] = total.astype(BF)
        for k in (2, 1, 3):
            ag_copy(gran, row, n, k).start()

    def spread(gran, row, n):
        for k in (1, 3, 2):
            ag_arrival(gran, row, n, k).wait_recv()
        half_copy(gran, row, n, core).start()

    def finish(gran, row, n):
        half_copy(gran, row, n, 1 - core).wait_recv()

    def store(slot, row, n):
        rows = rows_at(row, n)
        return pltpu.make_async_copy(rbuf.at[rows], r_hbm.at[rows], out_sem.at[slot])

    def store_gradient(slot, half, first, n):
        part = pl.ds(first, n)
        return pltpu.make_async_copy((gx, gy)[half].at[part], gt_hbm.at[half, part], out_sem.at[slot])

    def sent(gran, row, n):
        swap(gran, row, n).wait_send()
        half_copy(gran, row, n, core).wait_send()
        for k in (1, 2, 3):
            rs_copy(gran, row, n, k).wait_send()
            ag_copy(gran, row, n, k).wait_send()

    GH = FEAT // 2
    GQ = FEAT // 4

    def gg(phase, k):
        fwd = k % 4 >= 2
        minus = k % 2
        is_y = k >= 4
        buf = gy if is_y else gx
        if phase == 0:
            dev = ((yp, ym) if is_y else (xp, xm))[minus]
            if fwd:
                rows = pl.ds(GQ * minus, GQ)
                src, dst = buf.at[0, 1 + minus, rows], buf.at[0, 3, rows]
            else:
                src, dst = buf.at[0, 0], buf.at[0, 1 + minus]
        else:
            dev = ((xp, xm) if is_y else (yp, ym))[minus]
            if fwd:
                one = 2 * (phase - 1) + minus
                src, dst = buf.at[1 + minus, one], buf.at[3, one]
            else:
                part = pl.ds(2 * (phase - 1), 2)
                src, dst = buf.at[0, part], buf.at[1 + minus, part]
        sem = 8 * phase + k
        return remote(src, dst, gg_send.at[sem], gg_recv.at[sem], dev)

    def gr_swap():
        return remote(gpart.at[1 - core], gcrecv, gr_send.at[0], gr_recv.at[0], partner)

    def gr_copy(k):
        return remote(gpart.at[core, lax.rem(z + k, 4)], gzrecv.at[k - 1], gr_send.at[k], gr_recv.at[k], zpeer(k))

    loads[0].wait()
    loads[1].wait()
    for half, i in ((0, 0), (1, 4)):
        g = gate_v[pl.ds(half * HALF, HALF), :].astype(F32)
        u = up_v[pl.ds(half * HALF, HALF), :].astype(F32)
        abuf[pl.ds(i * HALF, HALF), :] = (g / (1.0 + jnp.exp(-g)) * u).astype(BF)
        for k in (0, 1):
            xy(-1, 4 * half + k).start()
        if half == 0:
            for c in loads[2:]:
                c.start()

    loads[2].wait()
    loads[3].wait()

    def rotate(c, carry):
        cols = pl.ds(pl.multiple_of(c * FEAT, 128), FEAT)
        gpart[lax.rem(c, 2), lax.div(c, 2)] = jnp.dot(grad_v[...], bout_v[:, cols], preferred_element_type=F32)
        return carry

    lax.fori_loop(0, NT, rotate, 0)
    gr_swap().start()
    for k in (0, 1, 4, 5):
        xy(0, k).start()
    gr_swap().wait_recv()
    for k in (2, 1, 3):
        there = lax.rem(z + k, 4)
        gpart[core, there] = gpart[core, there] + gcrecv[there]
        gr_copy(k).start()
    loads[4].wait()

    for k in (0, 1, 4, 5):
        xy(-1, k).wait_recv()
        xy(-1, k + 2).start()
    for k in (0, 1, 4, 5):
        xy(1, k).start()

    def near_of(j):
        return (2 + 2 * j, OWN * HALF + j * (PER * HALF), 256)

    def far_of(j):
        return (3 + 2 * j, OWN * HALF + j * (PER * HALF) + 256, 128)

    own = ((0, 0, 256), (1, 256, 256))

    def step(j, carry):
        for k in (0, 1, 4, 5):
            xy(j, k).wait_recv()
            xy(j, k + 2).start()

        @pl.when(j < 2)
        def _():
            @pl.when(j == 1)
            def _():
                for k in (0, 1, 4, 5):
                    gg(0, k).start()

            for k in (0, 1, 4, 5):
                xy(j + 2, k).start()

        @pl.when(j == 2)
        def _():
            for k in (0, 1, 4, 5):
                gg(0, k).wait_recv()
                gg(0, k + 2).start()

        @pl.when(j == 3)
        def _():
            for k in (2, 3, 6, 7):
                gg(0, k).wait_recv()
            for phase in (1, 2):
                for k in (0, 1, 4, 5):
                    gg(phase, k).start()

        multiply(*near_of(j))

        @pl.when(j == 1)
        def _():
            for g in own:
                combine(*g)

        @pl.when(j > 1)
        def _():
            combine(*far_of(j - 2))

        @pl.when(j > 0)
        def _():
            spread(*near_of(j - 1))

        pair(*near_of(j))

        @pl.when(j == 0)
        def _():
            for k in (2, 3, 6, 7):
                xy(-1, k).wait_recv()
            lax.fori_loop(0, 2, lambda g, c: (multiply(g, g * 256, 256), c)[1], 0)
            for g in own:
                pair(*g)

        @pl.when(j > 0)
        def _():
            for k in (2, 3, 6, 7):
                xy(j - 1, k).wait_recv()
            multiply(*far_of(j - 1))
            pair(*far_of(j - 1))

        combine(*near_of(j))

        @pl.when(j == 0)
        def _():
            share = gpart[core, z] + gcrecv[z]
            for k in (1, 3, 2):
                gr_copy(k).wait_recv()
                share = share + gzrecv[k - 1]
            share = share.T.astype(BF)
            gx[0, 0] = share[:GH]
            gy[0, 0] = share[GH:]

        @pl.when(j == 1)
        def _():
            for g in own:
                spread(*g)
            for k in range(8):
                xy(-1, k).wait_send()
            gr_swap().wait_send()
            for k in (1, 2, 3):
                gr_copy(k).wait_send()

        @pl.when(j > 1)
        def _():
            spread(*far_of(j - 2))
            for k in range(8):
                xy(j - 2, k).wait_send()

        @pl.when(j == 2)
        def _():
            for g in own:
                finish(*g)
                sent(*g)
            store(0, 0, 512).start()

        @pl.when(j == 3)
        def _():
            for g in (near_of(0), far_of(0)):
                finish(*g)
                sent(*g)
            store(1, 512, 384).start()

        return carry

    lax.fori_loop(0, STEPS, step, 0)

    def forward(phase):
        for k in (0, 1, 4, 5):
            gg(phase, k).wait_recv()
            gg(phase, k + 2).start()

    for k in (2, 3, 6, 7):
        xy(3, k).wait_recv()
    multiply(*far_of(3))
    combine(*far_of(2))
    spread(*near_of(3))
    pair(*far_of(3))
    forward(1)
    for g in (near_of(1), far_of(1)):
        finish(*g)
    store(2, 512 + 384, 384).start()
    spread(*far_of(2))
    combine(*far_of(3))
    forward(2)
    for half in (0, 1):
        store_gradient(6 + half, half, 0, 3).start()
    for g in (near_of(2), far_of(2), near_of(3)):
        finish(*g)
    store(3, 512 + 768, 384 + 256).start()
    for g in (near_of(1), far_of(1), near_of(2)):
        sent(*g)
    for j in (2, 3):
        for k in range(8):
            xy(j, k).wait_send()
    for k in range(8):
        gg(0, k).wait_send()
    spread(*far_of(3))
    for g in (far_of(2), near_of(3)):
        sent(*g)
    for phase in (1, 2):
        for k in (2, 3, 6, 7):
            gg(phase, k).wait_recv()
    for half in (0, 1):
        store_gradient(8 + half, half, 3, 1).start()
    finish(*far_of(3))
    store(5, 2048 - 128, 128).start()
    sent(*far_of(3))
    for phase in (1, 2):
        for k in range(8):
            gg(phase, k).wait_send()
    store(0, 0, 512).wait()
    store(1, 512, 384).wait()
    store(2, 512 + 384, 384).wait()
    store(3, 512 + 768, 384 + 256).wait()
    store(5, 2048 - 128, 128).wait()
    for half in (0, 1):
        store_gradient(6 + half, half, 0, 3).wait()
        store_gradient(8 + half, half, 3, 1).wait()


def gather_call(gate, up, grad, basis_in, basis_out):
    vm = pltpu.VMEM
    dma = pltpu.SemaphoreType.DMA
    hbm = pl.BlockSpec(memory_space=pl.ANY)
    return pl.pallas_call(
        gather_kernel,
        out_shape=(
            jax.ShapeDtypeStruct((2048, COLS), BF),
            jax.ShapeDtypeStruct((2, 4, 4, FEAT // 2, TOK), BF),
        ),
        in_specs=[hbm] * 5,
        out_specs=(hbm, hbm),
        scratch_shapes=[
            vm((TOK, HID), BF), vm((TOK, HID), BF), vm((TOK, FEAT), BF), vm((HID, COLS), BF), vm((FEAT, D), BF),
            vm((2048, HID), BF), vm((2048, COLS), F32), vm((1024, COLS), F32), vm((1024, COLS), BF),
            vm((3, 256, COLS), BF), vm((2048, COLS), BF),
            vm((2, 4, TOK, FEAT), F32), vm((4, TOK, FEAT), F32), vm((3, TOK, FEAT), F32),
            vm((4, 4, FEAT // 2, TOK), BF), vm((4, 4, FEAT // 2, TOK), BF),
            dma((5,)), dma((40,)), dma((40,)), dma((10,)), dma((10,)), dma((10, 3)), dma((10, 3)),
            dma((10, 3)), dma((10, 3)), dma((10,)), dma((10,)),
            dma((4,)), dma((4,)), dma((24,)), dma((24,)), dma((10,)),
        ],
        compiler_params=pltpu.CompilerParams(
            collective_id=0, has_side_effects=True, vmem_limit_bytes=58 * 2**20
        ),
        name="rotate_gather",
    )(gate, up, grad, basis_in, basis_out)


KB = 256
NB = 896


def fit_kernel(lengths, r_ref, gt_ref, out_ref):
    gi = lax.axis_index("grid")
    x = lax.div(gi, 4) * 2 + lax.axis_index("batch")
    y = lax.rem(gi, 4)

    def code(there, here):
        d = lax.rem(there - here + 4, 4)
        return jnp.where(d == 0, 0, jnp.where(d == 3, 1, d + 1))

    def codes(block):
        bx = lax.rem(lax.div(block, 4), 2) * 2 + lax.div(block, 8)
        return code(bx, x), code(lax.rem(block, 4), y)

    def rows_of(cx, cy, half):
        a, b = (cx, cy) if half == 0 else (cy, cx)
        near = jnp.where(b == 3, 4 + half, b - 1 + 2 * half)
        i = jnp.where(b == 0, a + 4 * half, OWN + PER * a + near)
        return r_ref[pl.ds(pl.multiple_of(i * HALF, HALF), HALF), :]

    out_ref[...] = jnp.zeros_like(out_ref)

    def add(s, begin):
        end = begin + lengths[s]
        first = lax.div(begin, KB)
        blocks = lax.div(end + KB - 1, KB) - first

        for n in (1, 2, 3):

            @pl.when(blocks == n)
            def _():
                rs, gs = [], []
                for i in range(2 * n):
                    cx, cy = codes(2 * first + i)
                    rs += [rows_of(cx, cy, 0), rows_of(cx, cy, 1)]
                    gs.append(jnp.concatenate([gt_ref[0, cy, cx], gt_ref[1, cx, cy]], axis=0))
                r = jnp.concatenate(rs, axis=0)
                token = first * KB + lax.broadcasted_iota(jnp.int32, r.shape, 0)
                r = jnp.where((token >= begin) & (token < end), r, jnp.zeros_like(r))
                p = jnp.dot(jnp.concatenate(gs, axis=1), r, preferred_element_type=F32)
                out_ref[...] += p * p

        return end

    lax.fori_loop(0, 8, add, 0)
    out_ref[...] = out_ref[...] * 0.125


def fit_call(lengths, r, gt):
    return pl.pallas_call(
        fit_kernel,
        grid=(pl.cdiv(COLS, NB),),
        out_shape=jax.ShapeDtypeStruct((FEAT, COLS), F32),
        in_specs=[
            pl.BlockSpec(memory_space=pltpu.SMEM),
            pl.BlockSpec((2048, NB), lambda i: (0, i)),
            pl.BlockSpec(memory_space=pltpu.VMEM),
        ],
        out_specs=pl.BlockSpec((FEAT, NB), lambda i: (0, i)),
        compiler_params=pltpu.CompilerParams(vmem_limit_bytes=58 * 2**20),
        name="sequence_products",
    )(lengths, r, gt)


def shards(gate_pre, up_pre, out_grad, basis_in, basis_out, lengths):
    r, gt = gather_call(gate_pre, up_pre, out_grad, basis_in, basis_out)
    return fit_call(lengths, r, gt)


def solution(mesh):
    return jax.shard_map(
        shards,
        mesh=mesh,
        in_specs=(
            P(("batch", "grid"), "tensor"),
            P(("batch", "grid"), "tensor"),
            P(("batch", "grid"), "tensor"),
            P("tensor", ("batch", "grid")),
            P("tensor", None),
            P(),
        ),
        out_specs=P("tensor", ("batch", "grid")),
        check_vma=False,
    )
```

```python
import functools

import jax
import jax.numpy as jnp
from jax import lax
from jax.experimental import pallas as pl
from jax.experimental.pallas import tpu as pltpu
from jax.sharding import PartitionSpec as P

MESH = pl.DeviceIdType.MESH
BF = jnp.bfloat16
F32 = jnp.float32

TOK = 128
HALF = 64
QUART = 32
HID = 3456
COLS = 896
FEAT = 640
D = 5120
NT = 8
STEPS = 4
OWN = 8
PER = 6


def gather_kernel(
    gate_hbm, up_hbm, grad_hbm, bin_hbm, bout_hbm, r_hbm, gt_hbm,
    gate_v, up_v, grad_v, bin_v, bout_v,
    abuf, pbuf, crecv, zsend, zrecv, rbuf, gpart, gcrecv, gzrecv, gx, gy,
    load_sem, xy_send, xy_recv, ce_send, ce_recv, rs_send, rs_recv, ag_send, ag_recv, cf_send, cf_recv,
    gr_send, gr_recv, gg_send, gg_recv, out_sem,
):
    xl = lax.axis_index("batch")
    me = lax.axis_index("tensor")
    gi = lax.axis_index("grid")
    x = lax.div(gi, 4) * 2 + xl
    y = lax.rem(gi, 4)
    z = lax.div(me, 2)
    core = lax.rem(me, 2)

    def at(dx, dy):
        xx = lax.rem(x + (dx + 4), 4)
        yy = lax.rem(y + (dy + 4), 4)
        return (lax.rem(xx, 2), me, lax.div(xx, 2) * 4 + yy)

    def block_of(dx, dy):
        b, _, g = at(dx, dy)
        return b * 8 + g

    def zpeer(k):
        return (xl, lax.rem(z + k, 4) * 2 + core, gi)

    partner = (xl, z * 2 + 1 - core, gi)
    xp, xm, yp, ym = at(1, 0), at(-1, 0), at(0, 1), at(0, -1)

    loads = [
        pltpu.make_async_copy(s, d, load_sem.at[i])
        for i, (s, d) in enumerate(
            [(gate_hbm, gate_v), (up_hbm, up_v), (grad_hbm, grad_v), (bout_hbm, bout_v), (bin_hbm, bin_v)]
        )
    ]
    loads[0].start()
    loads[1].start()

    barrier = pltpu.get_barrier_semaphore()
    for dev in [xp, xm, yp, ym, partner, zpeer(1), zpeer(2), zpeer(3)]:
        pl.semaphore_signal(barrier, inc=1, device_id=dev, device_id_type=MESH)
    pl.semaphore_wait(barrier, 8)

    def remote(src, dst, ss, rs, dev):
        return pltpu.make_async_remote_copy(
            src_ref=src, dst_ref=dst, send_sem=ss, recv_sem=rs, device_id=dev, device_id_type=MESH
        )

    def rows_at(i, n):
        return pl.ds(pl.multiple_of(i, 16), n)

    def piece(i, off=0, n=HALF):
        return abuf.at[rows_at(i * HALF + off, n)]

    def xy(step, k, part=0):
        first = isinstance(step, int) and step < 0
        fwd = k % 4 >= 2
        minus = k % 2
        is_y = k >= 4
        if first:
            base = 4 if is_y else 0
            own, near, far = base, base + 1 + minus, base + 3
            dev = ((yp, ym) if is_y else (xp, xm))[minus]
        else:
            b = OWN + PER * step
            own = (4 if is_y else 0) + step
            near = b + (2 if is_y else 0) + minus
            far = b + 4 + (1 if is_y else 0)
            dev = ((xp, xm) if is_y else (yp, ym))[minus]
        if fwd:
            src, dst = piece(near, QUART * minus, QUART), piece(far, QUART * minus, QUART)
        elif first:
            src, dst = piece(own, QUART * part, QUART), piece(near, QUART * part, QUART)
        else:
            src, dst = piece(own), piece(near)
        sem = (k + 40 * part if first else 8 + 8 * step + k)
        return remote(src, dst, xy_send.at[sem], xy_recv.at[sem], dev)

    def swap(gran, row, n):
        h = n // 2
        return remote(
            pbuf.at[rows_at(row + (1 - core) * h, h)], crecv.at[rows_at(lax.div(row, 2), h)],
            ce_send.at[gran], ce_recv.at[gran], partner,
        )

    def rs_copy(gran, row, n, k):
        m = n // 8
        return remote(
            zsend.at[rows_at(lax.div(row, 2) + lax.rem(z + k, 4) * m, m)],
            zrecv.at[k - 1, rows_at(lax.div(row, 8), m)],
            rs_send.at[gran, k - 1], rs_recv.at[gran, k - 1], zpeer(k),
        )

    def ag_copy(gran, row, n, k):
        m = n // 8
        here = rbuf.at[rows_at(row + core * (n // 2) + z * m, m)]
        return remote(here, here, ag_send.at[gran, k - 1], ag_recv.at[gran, k - 1], zpeer(k))

    def ag_arrival(gran, row, n, k):
        m = n // 8
        there = rbuf.at[rows_at(row + core * (n // 2) + lax.rem(z + 4 - k, 4) * m, m)]
        return remote(there, there, ag_send.at[gran, k - 1], ag_recv.at[gran, k - 1], zpeer(k))

    def half_copy(gran, row, n, c):
        there = rbuf.at[rows_at(row + c * (n // 2), n // 2)]
        return remote(there, there, cf_send.at[gran], cf_recv.at[gran], partner)

    def multiply(gran, row, n):
        rows = rows_at(row, n)
        pbuf[rows, :] = jnp.dot(abuf[rows, :], bin_v[...], preferred_element_type=F32)
        swap(gran, row, n).start()

    def pair(gran, row, n):
        h = n // 2
        swap(gran, row, n).wait_recv()
        mine = pbuf[rows_at(row + core * h, h), :]
        theirs = crecv[rows_at(lax.div(row, 2), h), :]
        zsend[rows_at(lax.div(row, 2), h), :] = (mine + theirs).astype(BF)
        for k in (2, 1, 3):
            rs_copy(gran, row, n, k).start()

    def combine(gran, row, n):
        h, m = n // 2, n // 8
        total = pbuf[rows_at(row + core * h + z * m, m), :] + crecv[rows_at(lax.div(row, 2) + z * m, m), :]
        for k in (1, 3, 2):
            rs_copy(gran, row, n, k).wait_recv()
            total = total + zrecv[k - 1, rows_at(lax.div(row, 8), m), :].astype(F32)
        rbuf[rows_at(row + core * h + z * m, m), :] = total.astype(BF)
        for k in (2, 1, 3):
            ag_copy(gran, row, n, k).start()

    def spread(gran, row, n):
        for k in (1, 3, 2):
            ag_arrival(gran, row, n, k).wait_recv()
        half_copy(gran, row, n, core).start()

    def finish(gran, row, n):
        half_copy(gran, row, n, 1 - core).wait_recv()

    def store(i, cx, cy, half):
        return pltpu.make_async_copy(
            rbuf.at[rows_at(i * HALF, HALF)], r_hbm.at[cx, cy, pl.ds(half * HALF, HALF)], out_sem.at[i]
        )

    def store_own():
        return [store(i, i, 0, 0) for i in range(4)] + [store(4 + i, 0, i, 1) for i in range(4)]

    def store_near(j):
        b = OWN + PER * j
        return [store(b, j, 1, 0), store(b + 1, j, 2, 0), store(b + 2, 1, j, 1), store(b + 3, 2, j, 1)]

    def store_far(j):
        b = OWN + PER * j
        return [store(b + 4, j, 3, 0), store(b + 5, 3, j, 1)]

    def store_gradient(i):
        return [
            pltpu.make_async_copy(gx.at[i], gt_hbm.at[:, i, pl.ds(0, GH)], out_sem.at[32 + i]),
            pltpu.make_async_copy(gy.at[i], gt_hbm.at[i, :, pl.ds(GH, GH)], out_sem.at[36 + i]),
        ]

    def start(copies):
        for c in copies:
            c.start()

    def sent(gran, row, n):
        swap(gran, row, n).wait_send()
        half_copy(gran, row, n, core).wait_send()
        for k in (1, 2, 3):
            rs_copy(gran, row, n, k).wait_send()
            ag_copy(gran, row, n, k).wait_send()

    GH = FEAT // 2
    GQ = FEAT // 4

    def gg(phase, k):
        fwd = k % 4 >= 2
        minus = k % 2
        is_y = k >= 4
        buf = gy if is_y else gx
        if phase == 0:
            dev = ((yp, ym) if is_y else (xp, xm))[minus]
            if fwd:
                rows = pl.ds(GQ * minus, GQ)
                src, dst = buf.at[0, 1 + minus, rows], buf.at[0, 3, rows]
            else:
                src, dst = buf.at[0, 0], buf.at[0, 1 + minus]
        else:
            dev = ((xp, xm) if is_y else (yp, ym))[minus]
            if fwd:
                one = 2 * (phase - 1) + minus
                src, dst = buf.at[1 + minus, one], buf.at[3, one]
            else:
                part = pl.ds(2 * (phase - 1), 2)
                src, dst = buf.at[0, part], buf.at[1 + minus, part]
        sem = 8 * phase + k
        return remote(src, dst, gg_send.at[sem], gg_recv.at[sem], dev)

    def gr_swap():
        return remote(gpart.at[1 - core], gcrecv, gr_send.at[0], gr_recv.at[0], partner)

    def gr_copy(k):
        return remote(gpart.at[core, lax.rem(z + k, 4)], gzrecv.at[k - 1], gr_send.at[k], gr_recv.at[k], zpeer(k))

    loads[0].wait()
    loads[1].wait()
    for part in (0, 1):
        for half, i in ((0, 0), (1, 4)):
            rows = pl.ds(half * HALF + part * QUART, QUART)
            g = gate_v[rows, :].astype(F32)
            u = up_v[rows, :].astype(F32)
            abuf[pl.ds(i * HALF + part * QUART, QUART), :] = (g / (1.0 + jnp.exp(-g)) * u).astype(BF)
            for k in (0, 1):
                xy(-1, 4 * half + k, part).start()
            if part == 0 and half == 1:
                for c in loads[2:]:
                    c.start()

    loads[2].wait()
    loads[3].wait()

    def rotate(c, carry):
        cols = pl.ds(pl.multiple_of(c * FEAT, 128), FEAT)
        gpart[lax.rem(c, 2), lax.div(c, 2)] = jnp.dot(grad_v[...], bout_v[:, cols], preferred_element_type=F32)
        return carry

    lax.fori_loop(0, NT, rotate, 0)
    gr_swap().start()
    for k in (0, 1, 4, 5):
        xy(0, k).start()
    gr_swap().wait_recv()
    for k in (2, 1, 3):
        there = lax.rem(z + k, 4)
        gpart[core, there] = gpart[core, there] + gcrecv[there]
        gr_copy(k).start()
    loads[4].wait()

    for k in (0, 1, 4, 5):
        for part in (0, 1):
            xy(-1, k, part).wait_recv()
        xy(-1, k + 2).start()
    for k in (0, 1, 4, 5):
        xy(1, k).start()

    def near_of(j):
        return (2 + 2 * j, OWN * HALF + j * (PER * HALF), 256)

    def far_of(j):
        return (3 + 2 * j, OWN * HALF + j * (PER * HALF) + 256, 128)

    own = ((0, 0, 256), (1, 256, 256))

    def step(j, carry):
        for k in (0, 1, 4, 5):
            xy(j, k).wait_recv()
            xy(j, k + 2).start()

        @pl.when(j < 2)
        def _():
            @pl.when(j == 1)
            def _():
                for k in (0, 1, 4, 5):
                    gg(0, k).start()

            for k in (0, 1, 4, 5):
                xy(j + 2, k).start()

        @pl.when(j == 2)
        def _():
            for k in (0, 1, 4, 5):
                gg(0, k).wait_recv()
                gg(0, k + 2).start()

        @pl.when(j == 3)
        def _():
            for k in (2, 3, 6, 7):
                gg(0, k).wait_recv()
            for phase in (1, 2):
                for k in (0, 1, 4, 5):
                    gg(phase, k).start()

        multiply(*near_of(j))

        @pl.when(j == 1)
        def _():
            for g in own:
                combine(*g)

        @pl.when(j > 1)
        def _():
            combine(*far_of(j - 2))

        @pl.when(j > 0)
        def _():
            spread(*near_of(j - 1))

        pair(*near_of(j))

        @pl.when(j == 0)
        def _():
            for k in (2, 3, 6, 7):
                xy(-1, k).wait_recv()
            lax.fori_loop(0, 2, lambda g, c: (multiply(g, g * 256, 256), c)[1], 0)
            for g in own:
                pair(*g)

        @pl.when(j > 0)
        def _():
            for k in (2, 3, 6, 7):
                xy(j - 1, k).wait_recv()
            multiply(*far_of(j - 1))
            pair(*far_of(j - 1))

        combine(*near_of(j))

        @pl.when(j == 0)
        def _():
            share = gpart[core, z] + gcrecv[z]
            for k in (1, 3, 2):
                gr_copy(k).wait_recv()
                share = share + gzrecv[k - 1]
            share = share.T.astype(BF)
            gx[0, 0] = share[:GH]
            gy[0, 0] = share[GH:]

        @pl.when(j == 1)
        def _():
            for g in own:
                spread(*g)
            for k in range(8):
                xy(-1, k).wait_send()
            for k in (0, 1, 4, 5):
                xy(-1, k, 1).wait_send()
            gr_swap().wait_send()
            for k in (1, 2, 3):
                gr_copy(k).wait_send()

        @pl.when(j > 1)
        def _():
            spread(*far_of(j - 2))
            for k in range(8):
                xy(j - 2, k).wait_send()

        @pl.when(j == 2)
        def _():
            for g in own:
                finish(*g)
                sent(*g)
            start(store_own())

        @pl.when(j == 3)
        def _():
            for g in (near_of(0), far_of(0)):
                finish(*g)
                sent(*g)
            start(store_near(0) + store_far(0))

        return carry

    lax.fori_loop(0, STEPS, step, 0)

    def forward(phase):
        for k in (0, 1, 4, 5):
            gg(phase, k).wait_recv()
            gg(phase, k + 2).start()

    for k in (2, 3, 6, 7):
        xy(3, k).wait_recv()
    multiply(*far_of(3))
    pair(*far_of(3))
    combine(*far_of(2))
    forward(1)
    spread(*near_of(3))
    combine(*far_of(3))
    forward(2)
    spread(*far_of(2))
    start(store_gradient(1) + store_gradient(2))
    for g in (far_of(2), near_of(3)):
        finish(*g)
    start(store_far(2) + store_near(3))
    for g in (near_of(1), near_of(2)):
        finish(*g)
    start(store_near(1) + store_near(2))
    spread(*far_of(3))
    finish(*far_of(1))
    start(store_far(1) + store_gradient(0))
    for g in (near_of(1), far_of(1), near_of(2), far_of(2), near_of(3)):
        sent(*g)
    for j in (2, 3):
        for k in range(8):
            xy(j, k).wait_send()
    for k in range(8):
        gg(0, k).wait_send()
    for phase in (1, 2):
        for k in (2, 3, 6, 7):
            gg(phase, k).wait_recv()
    start(store_gradient(3))
    finish(*far_of(3))
    start(store_far(3))
    for phase in (1, 2):
        for k in range(8):
            gg(phase, k).wait_send()
    sent(*far_of(3))
    done = store_own()
    for j in range(STEPS):
        done += store_near(j) + store_far(j) + store_gradient(j)
    for c in done:
        c.wait()


def gather_call(gate, up, grad, basis_in, basis_out):
    vm = pltpu.VMEM
    dma = pltpu.SemaphoreType.DMA
    hbm = pl.BlockSpec(memory_space=pl.ANY)
    return pl.pallas_call(
        gather_kernel,
        out_shape=(
            jax.ShapeDtypeStruct((4, 4, TOK, COLS), BF),
            jax.ShapeDtypeStruct((4, 4, FEAT, TOK), BF),
        ),
        in_specs=[hbm] * 5,
        out_specs=(hbm, hbm),
        scratch_shapes=[
            vm((TOK, HID), BF), vm((TOK, HID), BF), vm((TOK, FEAT), BF), vm((HID, COLS), BF), vm((FEAT, D), BF),
            vm((2048, HID), BF), vm((2048, COLS), F32), vm((1024, COLS), F32), vm((1024, COLS), BF),
            vm((3, 256, COLS), BF), vm((2048, COLS), BF),
            vm((2, 4, TOK, FEAT), F32), vm((4, TOK, FEAT), F32), vm((3, TOK, FEAT), F32),
            vm((4, 4, FEAT // 2, TOK), BF), vm((4, 4, FEAT // 2, TOK), BF),
            dma((5,)), dma((48,)), dma((48,)), dma((10,)), dma((10,)), dma((10, 3)), dma((10, 3)),
            dma((10, 3)), dma((10, 3)), dma((10,)), dma((10,)),
            dma((4,)), dma((4,)), dma((24,)), dma((24,)), dma((40,)),
        ],
        compiler_params=pltpu.CompilerParams(
            collective_id=0, has_side_effects=True, vmem_limit_bytes=58 * 2**20
        ),
        name="rotate_gather",
    )(gate, up, grad, basis_in, basis_out)


KB = 128
CUTS = ((0, 256), (256, 256), (512, 256), (768, 128))


def fit_kernel(lengths, r_hbm, gt_hbm, out_hbm, r_ref, g_ref, acc, in_sem, out_sem):
    gi = lax.axis_index("grid")
    x = lax.div(gi, 4) * 2 + lax.axis_index("batch")
    y = lax.rem(gi, 4)

    def code(there, here):
        d = lax.rem(there - here + 4, 4)
        return jnp.where(d == 0, 0, jnp.where(d == 3, 1, d + 1))

    def load(quarter):
        cx = code(lax.rem(quarter, 2) * 2 + lax.div(quarter, 2), x)
        return (
            pltpu.make_async_copy(r_hbm.at[cx], r_ref.at[quarter], in_sem.at[quarter, 0]),
            pltpu.make_async_copy(gt_hbm.at[cx], g_ref.at[quarter], in_sem.at[quarter, 1]),
        )

    for quarter in range(4):
        for c in load(quarter):
            c.start()
    acc[...] = jnp.zeros_like(acc)

    def results(c):
        cols = pl.ds(*CUTS[c])
        return pltpu.make_async_copy(acc.at[:, cols], out_hbm.at[:, cols], out_sem.at[c])

    def add(s, begin):
        end = begin + lengths[s]
        first = lax.div(begin, KB)
        blocks = lax.div(end + KB - 1, KB) - first

        @pl.when(s < 4)
        def _():
            for c in load(s):
                c.wait()

        for n in range(1, 2 + 512 // KB):

            def factors():
                rs, gs = [], []
                for i in range(n * KB // 128):
                    block = first * (KB // 128) + i
                    quarter, cy = lax.div(block, 4), code(lax.rem(block, 4), y)
                    rs.append(r_ref[quarter, cy])
                    gs.append(g_ref[quarter, cy])
                r = jnp.concatenate(rs, axis=0)
                token = first * KB + lax.broadcasted_iota(jnp.int32, r.shape, 0)
                r = jnp.where((token >= begin) & (token < end), r, jnp.zeros_like(r))
                return jnp.concatenate(gs, axis=1), r

            @pl.when((blocks == n) & (s < 7))
            def _():
                g, r = factors()
                p = jnp.dot(g, r, preferred_element_type=F32)
                acc[...] += p * p

            @pl.when((blocks == n) & (s == 7))
            def _():
                g, r = factors()
                for c, (at, wide) in enumerate(CUTS):
                    cols = pl.ds(at, wide)
                    p = jnp.dot(g, r[:, at : at + wide], preferred_element_type=F32)
                    acc[:, cols] = (acc[:, cols] + p * p) * 0.125
                    results(c).start()

        return end

    lax.fori_loop(0, 8, add, 0)
    for c in range(len(CUTS)):
        results(c).wait()


def fit_call(lengths, r, gt):
    hbm = pl.BlockSpec(memory_space=pl.ANY)
    return pl.pallas_call(
        fit_kernel,
        out_shape=jax.ShapeDtypeStruct((FEAT, COLS), F32),
        in_specs=[pl.BlockSpec(memory_space=pltpu.SMEM), hbm, hbm],
        out_specs=hbm,
        scratch_shapes=[
            pltpu.VMEM((4, 4, 128, COLS), BF), pltpu.VMEM((4, 4, FEAT, 128), BF), pltpu.VMEM((FEAT, COLS), F32),
            pltpu.SemaphoreType.DMA((4, 2)), pltpu.SemaphoreType.DMA((4,)),
        ],
        compiler_params=pltpu.CompilerParams(vmem_limit_bytes=58 * 2**20),
        name="sequence_products",
    )(lengths, r, gt)


def shards(gate_pre, up_pre, out_grad, basis_in, basis_out, lengths):
    r, gt = gather_call(gate_pre, up_pre, out_grad, basis_in, basis_out)
    return fit_call(lengths, r, gt)


def solution(mesh):
    return jax.shard_map(
        shards,
        mesh=mesh,
        in_specs=(
            P(("batch", "grid"), "tensor"),
            P(("batch", "grid"), "tensor"),
            P(("batch", "grid"), "tensor"),
            P("tensor", ("batch", "grid")),
            P("tensor", None),
            P(),
        ),
        out_specs=P("tensor", ("batch", "grid")),
        check_vma=False,
    )
```

```python
import functools

import jax
import jax.numpy as jnp
from jax import lax
from jax.experimental import pallas as pl
from jax.experimental.pallas import tpu as pltpu
from jax.sharding import PartitionSpec as P

MESH = pl.DeviceIdType.MESH
BF = jnp.bfloat16
F32 = jnp.float32

TOK = 128
HALF = 64
QUART = 32
HID = 3456
COLS = 896
FEAT = 640
D = 5120
NT = 8
STEPS = 4
OWN = 8
PER = 6


def gather_kernel(
    gate_hbm, up_hbm, grad_hbm, bin_hbm, bout_hbm, r_hbm, gt_hbm,
    gate_v, up_v, grad_v, bin_v, bout_v,
    abuf, pbuf, crecv, zsend, zrecv, rbuf, gpart, gcrecv, gzrecv, gx, gy,
    load_sem, xy_send, xy_recv, ce_send, ce_recv, rs_send, rs_recv, ag_send, ag_recv, cf_send, cf_recv,
    gr_send, gr_recv, gg_send, gg_recv, out_sem,
):
    xl = lax.axis_index("batch")
    me = lax.axis_index("tensor")
    gi = lax.axis_index("grid")
    x = lax.div(gi, 4) * 2 + xl
    y = lax.rem(gi, 4)
    z = lax.div(me, 2)
    core = lax.rem(me, 2)

    def at(dx, dy):
        xx = lax.rem(x + (dx + 4), 4)
        yy = lax.rem(y + (dy + 4), 4)
        return (lax.rem(xx, 2), me, lax.div(xx, 2) * 4 + yy)

    def block_of(dx, dy):
        b, _, g = at(dx, dy)
        return b * 8 + g

    def zpeer(k):
        return (xl, lax.rem(z + k, 4) * 2 + core, gi)

    partner = (xl, z * 2 + 1 - core, gi)
    xp, xm, yp, ym = at(1, 0), at(-1, 0), at(0, 1), at(0, -1)

    loads = [
        pltpu.make_async_copy(s, d, load_sem.at[i])
        for i, (s, d) in enumerate(
            [(gate_hbm, gate_v), (up_hbm, up_v), (grad_hbm, grad_v), (bout_hbm, bout_v), (bin_hbm, bin_v)]
        )
    ]
    loads[0].start()
    loads[1].start()

    barrier = pltpu.get_barrier_semaphore()
    for dev in [xp, xm, yp, ym, partner, zpeer(1), zpeer(2), zpeer(3)]:
        pl.semaphore_signal(barrier, inc=1, device_id=dev, device_id_type=MESH)
    pl.semaphore_wait(barrier, 8)

    def remote(src, dst, ss, rs, dev):
        return pltpu.make_async_remote_copy(
            src_ref=src, dst_ref=dst, send_sem=ss, recv_sem=rs, device_id=dev, device_id_type=MESH
        )

    def rows_at(i, n):
        return pl.ds(pl.multiple_of(i, 16), n)

    def piece(i, off=0, n=HALF):
        return abuf.at[rows_at(i * HALF + off, n)]

    def xy(step, k, part=0):
        first = isinstance(step, int) and step < 0
        fwd = k % 4 >= 2
        minus = k % 2
        is_y = k >= 4
        if first:
            base = 4 if is_y else 0
            own, near, far = base, base + 1 + minus, base + 3
            dev = ((yp, ym) if is_y else (xp, xm))[minus]
        else:
            b = OWN + PER * step
            own = (4 if is_y else 0) + step
            near = b + (2 if is_y else 0) + minus
            far = b + 4 + (1 if is_y else 0)
            dev = ((xp, xm) if is_y else (yp, ym))[minus]
        if fwd:
            src, dst = piece(near, QUART * minus, QUART), piece(far, QUART * minus, QUART)
        elif first:
            src, dst = piece(own, QUART * part, QUART), piece(near, QUART * part, QUART)
        else:
            src, dst = piece(own), piece(near)
        sem = (k + 40 * part if first else 8 + 8 * step + k)
        return remote(src, dst, xy_send.at[sem], xy_recv.at[sem], dev)

    def swap(gran, row, n):
        h = n // 2
        return remote(
            pbuf.at[rows_at(row + (1 - core) * h, h)], crecv.at[rows_at(lax.div(row, 2), h)],
            ce_send.at[gran], ce_recv.at[gran], partner,
        )

    def rs_copy(gran, row, n, k):
        m = n // 8
        return remote(
            zsend.at[rows_at(lax.div(row, 2) + lax.rem(z + k, 4) * m, m)],
            zrecv.at[k - 1, rows_at(lax.div(row, 8), m)],
            rs_send.at[gran, k - 1], rs_recv.at[gran, k - 1], zpeer(k),
        )

    def ag_copy(gran, row, n, k):
        m = n // 8
        here = rbuf.at[rows_at(row + core * (n // 2) + z * m, m)]
        return remote(here, here, ag_send.at[gran, k - 1], ag_recv.at[gran, k - 1], zpeer(k))

    def ag_arrival(gran, row, n, k):
        m = n // 8
        there = rbuf.at[rows_at(row + core * (n // 2) + lax.rem(z + 4 - k, 4) * m, m)]
        return remote(there, there, ag_send.at[gran, k - 1], ag_recv.at[gran, k - 1], zpeer(k))

    def half_copy(gran, row, n, c):
        there = rbuf.at[rows_at(row + c * (n // 2), n // 2)]
        return remote(there, there, cf_send.at[gran], cf_recv.at[gran], partner)

    def multiply(gran, row, n):
        rows = rows_at(row, n)
        pbuf[rows, :] = jnp.dot(abuf[rows, :], bin_v[...], preferred_element_type=F32)
        swap(gran, row, n).start()

    def pair(gran, row, n):
        h = n // 2
        swap(gran, row, n).wait_recv()
        mine = pbuf[rows_at(row + core * h, h), :]
        theirs = crecv[rows_at(lax.div(row, 2), h), :]
        zsend[rows_at(lax.div(row, 2), h), :] = (mine + theirs).astype(BF)
        for k in (2, 1, 3):
            rs_copy(gran, row, n, k).start()

    def combine(gran, row, n):
        h, m = n // 2, n // 8
        total = pbuf[rows_at(row + core * h + z * m, m), :] + crecv[rows_at(lax.div(row, 2) + z * m, m), :]
        for k in (1, 3, 2):
            rs_copy(gran, row, n, k).wait_recv()
            total = total + zrecv[k - 1, rows_at(lax.div(row, 8), m), :].astype(F32)
        rbuf[rows_at(row + core * h + z * m, m), :] = total.astype(BF)
        for k in (2, 1, 3):
            ag_copy(gran, row, n, k).start()

    def spread(gran, row, n):
        for k in (1, 3, 2):
            ag_arrival(gran, row, n, k).wait_recv()
        half_copy(gran, row, n, core).start()

    def finish(gran, row, n):
        half_copy(gran, row, n, 1 - core).wait_recv()

    def store(i, cx, cy, half):
        return pltpu.make_async_copy(
            rbuf.at[rows_at(i * HALF, HALF)], r_hbm.at[cx, cy, pl.ds(half * HALF, HALF)], out_sem.at[i]
        )

    def store_own():
        return [store(i, i, 0, 0) for i in range(4)] + [store(4 + i, 0, i, 1) for i in range(4)]

    def store_near(j):
        b = OWN + PER * j
        return [store(b, j, 1, 0), store(b + 1, j, 2, 0), store(b + 2, 1, j, 1), store(b + 3, 2, j, 1)]

    def store_far(j):
        b = OWN + PER * j
        return [store(b + 4, j, 3, 0), store(b + 5, 3, j, 1)]

    def store_gradient(i):
        return [
            pltpu.make_async_copy(gx.at[i], gt_hbm.at[:, i, pl.ds(0, GH)], out_sem.at[32 + i]),
            pltpu.make_async_copy(gy.at[i], gt_hbm.at[i, :, pl.ds(GH, GH)], out_sem.at[36 + i]),
        ]

    def start(copies):
        for c in copies:
            c.start()

    def sent(gran, row, n):
        swap(gran, row, n).wait_send()
        half_copy(gran, row, n, core).wait_send()
        for k in (1, 2, 3):
            rs_copy(gran, row, n, k).wait_send()
            ag_copy(gran, row, n, k).wait_send()

    GH = FEAT // 2
    GQ = FEAT // 4

    def gg(phase, k):
        fwd = k % 4 >= 2
        minus = k % 2
        is_y = k >= 4
        buf = gy if is_y else gx
        if phase == 0:
            dev = ((yp, ym) if is_y else (xp, xm))[minus]
            if fwd:
                rows = pl.ds(GQ * minus, GQ)
                src, dst = buf.at[0, 1 + minus, rows], buf.at[0, 3, rows]
            else:
                src, dst = buf.at[0, 0], buf.at[0, 1 + minus]
        else:
            dev = ((xp, xm) if is_y else (yp, ym))[minus]
            if fwd:
                one = 2 * (phase - 1) + minus
                src, dst = buf.at[1 + minus, one], buf.at[3, one]
            else:
                part = pl.ds(2 * (phase - 1), 2)
                src, dst = buf.at[0, part], buf.at[1 + minus, part]
        sem = 8 * phase + k
        return remote(src, dst, gg_send.at[sem], gg_recv.at[sem], dev)

    def gr_swap():
        return remote(gpart.at[1 - core], gcrecv, gr_send.at[0], gr_recv.at[0], partner)

    def gr_copy(k):
        return remote(gpart.at[core, lax.rem(z + k, 4)], gzrecv.at[k - 1], gr_send.at[k], gr_recv.at[k], zpeer(k))

    loads[0].wait()
    loads[1].wait()
    for part in (0, 1):
        for half, i in ((0, 0), (1, 4)):
            rows = pl.ds(half * HALF + part * QUART, QUART)
            g = gate_v[rows, :].astype(F32)
            u = up_v[rows, :].astype(F32)
            abuf[pl.ds(i * HALF + part * QUART, QUART), :] = (g / (1.0 + jnp.exp(-g)) * u).astype(BF)
            for k in (0, 1):
                xy(-1, 4 * half + k, part).start()
            if part == 0 and half == 1:
                for c in loads[2:]:
                    c.start()

    loads[2].wait()
    loads[3].wait()

    def rotate(c, carry):
        cols = pl.ds(pl.multiple_of(c * FEAT, 128), FEAT)
        gpart[lax.rem(c, 2), lax.div(c, 2)] = jnp.dot(grad_v[...], bout_v[:, cols], preferred_element_type=F32)
        return carry

    lax.fori_loop(0, NT, rotate, 0)
    gr_swap().start()
    for k in (0, 1, 4, 5):
        xy(0, k).start()
    gr_swap().wait_recv()
    for k in (2, 1, 3):
        there = lax.rem(z + k, 4)
        gpart[core, there] = gpart[core, there] + gcrecv[there]
        gr_copy(k).start()
    loads[4].wait()

    for k in (0, 1, 4, 5):
        for part in (0, 1):
            xy(-1, k, part).wait_recv()
        xy(-1, k + 2).start()
    for k in (0, 1, 4, 5):
        xy(1, k).start()

    def near_of(j):
        return (2 + 2 * j, OWN * HALF + j * (PER * HALF), 256)

    def far_of(j):
        return (3 + 2 * j, OWN * HALF + j * (PER * HALF) + 256, 128)

    own = ((0, 0, 256), (1, 256, 256))

    def pass_on(j):
        for k in (0, 1, 4, 5):
            xy(j, k).wait_recv()
            xy(j, k + 2).start()

        @pl.when(j < 2)
        def _():
            for k in (0, 1, 4, 5):
                xy(j + 2, k).start()

        @pl.when(j == 2)
        def _():
            for k in (0, 1, 4, 5):
                gg(0, k).start()

        @pl.when(j == 3)
        def _():
            for k in (0, 1, 4, 5):
                gg(0, k).wait_recv()
                gg(0, k + 2).start()
                gg(1, k).start()

    def step(j, carry):
        pass_on(j)

        multiply(*near_of(j))

        @pl.when(j == 1)
        def _():
            for g in own:
                combine(*g)

        @pl.when(j > 1)
        def _():
            combine(*far_of(j - 2))

        @pl.when(j > 0)
        def _():
            spread(*near_of(j - 1))

        pair(*near_of(j))

        @pl.when(j == 0)
        def _():
            for k in (2, 3, 6, 7):
                xy(-1, k).wait_recv()
            lax.fori_loop(0, 2, lambda g, c: (multiply(g, g * 256, 256), c)[1], 0)
            for g in own:
                pair(*g)

        @pl.when(j > 0)
        def _():
            for k in (2, 3, 6, 7):
                xy(j - 1, k).wait_recv()
            multiply(*far_of(j - 1))
            pair(*far_of(j - 1))

        combine(*near_of(j))

        @pl.when(j == 0)
        def _():
            share = gpart[core, z] + gcrecv[z]
            for k in (1, 3, 2):
                gr_copy(k).wait_recv()
                share = share + gzrecv[k - 1]
            share = share.T.astype(BF)
            gx[0, 0] = share[:GH]
            gy[0, 0] = share[GH:]

        @pl.when(j == 1)
        def _():
            for g in own:
                spread(*g)
            for k in range(8):
                xy(-1, k).wait_send()
            for k in (0, 1, 4, 5):
                xy(-1, k, 1).wait_send()
            gr_swap().wait_send()
            for k in (1, 2, 3):
                gr_copy(k).wait_send()

        @pl.when(j > 1)
        def _():
            spread(*far_of(j - 2))
            for k in range(8):
                xy(j - 2, k).wait_send()

        @pl.when(j == 2)
        def _():
            for g in own:
                finish(*g)
                sent(*g)
            start(store_own())

        @pl.when(j == 3)
        def _():
            for g in (near_of(0), far_of(0)):
                finish(*g)
                sent(*g)
            start(store_near(0) + store_far(0))

        return carry

    lax.fori_loop(0, STEPS, step, 0)

    def forward(phase):
        for k in (0, 1, 4, 5):
            gg(phase, k).wait_recv()
            gg(phase, k + 2).start()

    for k in (2, 3, 6, 7):
        xy(3, k).wait_recv()
    multiply(*far_of(3))
    for k in (2, 3, 6, 7):
        gg(0, k).wait_recv()
    for k in (0, 1, 4, 5):
        gg(2, k).start()
    pair(*far_of(3))
    combine(*far_of(2))
    forward(1)
    spread(*near_of(3))
    combine(*far_of(3))
    forward(2)
    spread(*far_of(2))
    start(store_gradient(1) + store_gradient(2))
    for g in (far_of(2), near_of(3)):
        finish(*g)
    start(store_far(2) + store_near(3))
    for g in (near_of(1), near_of(2)):
        finish(*g)
    start(store_near(1) + store_near(2))
    spread(*far_of(3))
    finish(*far_of(1))
    start(store_far(1) + store_gradient(0))
    for g in (near_of(1), far_of(1), near_of(2), far_of(2), near_of(3)):
        sent(*g)
    for j in (2, 3):
        for k in range(8):
            xy(j, k).wait_send()
    for k in range(8):
        gg(0, k).wait_send()
    for phase in (1, 2):
        for k in (2, 3, 6, 7):
            gg(phase, k).wait_recv()
    start(store_gradient(3))
    finish(*far_of(3))
    start(store_far(3))
    for phase in (1, 2):
        for k in range(8):
            gg(phase, k).wait_send()
    sent(*far_of(3))
    done = store_own()
    for j in range(STEPS):
        done += store_near(j) + store_far(j) + store_gradient(j)
    for c in done:
        c.wait()


def gather_call(gate, up, grad, basis_in, basis_out):
    vm = pltpu.VMEM
    dma = pltpu.SemaphoreType.DMA
    hbm = pl.BlockSpec(memory_space=pl.ANY)
    return pl.pallas_call(
        gather_kernel,
        out_shape=(
            jax.ShapeDtypeStruct((4, 4, TOK, COLS), BF),
            jax.ShapeDtypeStruct((4, 4, FEAT, TOK), BF),
        ),
        in_specs=[hbm] * 5,
        out_specs=(hbm, hbm),
        scratch_shapes=[
            vm((TOK, HID), BF), vm((TOK, HID), BF), vm((TOK, FEAT), BF), vm((HID, COLS), BF), vm((FEAT, D), BF),
            vm((2048, HID), BF), vm((2048, COLS), F32), vm((1024, COLS), F32), vm((1024, COLS), BF),
            vm((3, 256, COLS), BF), vm((2048, COLS), BF),
            vm((2, 4, TOK, FEAT), F32), vm((4, TOK, FEAT), F32), vm((3, TOK, FEAT), F32),
            vm((4, 4, FEAT // 2, TOK), BF), vm((4, 4, FEAT // 2, TOK), BF),
            dma((5,)), dma((48,)), dma((48,)), dma((10,)), dma((10,)), dma((10, 3)), dma((10, 3)),
            dma((10, 3)), dma((10, 3)), dma((10,)), dma((10,)),
            dma((4,)), dma((4,)), dma((24,)), dma((24,)), dma((40,)),
        ],
        compiler_params=pltpu.CompilerParams(
            collective_id=0, has_side_effects=True, vmem_limit_bytes=58 * 2**20
        ),
        name="rotate_gather",
    )(gate, up, grad, basis_in, basis_out)


KB = 128
CUTS = ((0, 256), (256, 256), (512, 256), (768, 128))


def fit_kernel(lengths, r_hbm, gt_hbm, out_hbm, r_ref, g_ref, acc, in_sem, out_sem):
    gi = lax.axis_index("grid")
    x = lax.div(gi, 4) * 2 + lax.axis_index("batch")
    y = lax.rem(gi, 4)

    def code(there, here):
        d = lax.rem(there - here + 4, 4)
        return jnp.where(d == 0, 0, jnp.where(d == 3, 1, d + 1))

    def load(quarter):
        cx = code(lax.rem(quarter, 2) * 2 + lax.div(quarter, 2), x)
        return (
            pltpu.make_async_copy(r_hbm.at[cx], r_ref.at[quarter], in_sem.at[quarter, 0]),
            pltpu.make_async_copy(gt_hbm.at[cx], g_ref.at[quarter], in_sem.at[quarter, 1]),
        )

    for quarter in range(4):
        for c in load(quarter):
            c.start()
    acc[...] = jnp.zeros_like(acc)

    def results(c):
        cols = pl.ds(*CUTS[c])
        return pltpu.make_async_copy(acc.at[:, cols], out_hbm.at[:, cols], out_sem.at[c])

    def add(s, begin):
        end = begin + lengths[s]
        first = lax.div(begin, KB)
        blocks = lax.div(end + KB - 1, KB) - first

        @pl.when(s < 4)
        def _():
            for c in load(s):
                c.wait()

        for n in range(1, 2 + 512 // KB):

            def factors():
                rs, gs = [], []
                for i in range(n * KB // 128):
                    block = first * (KB // 128) + i
                    quarter, cy = lax.div(block, 4), code(lax.rem(block, 4), y)
                    rs.append(r_ref[quarter, cy])
                    gs.append(g_ref[quarter, cy])
                r = jnp.concatenate(rs, axis=0)
                token = first * KB + lax.broadcasted_iota(jnp.int32, r.shape, 0)
                r = jnp.where((token >= begin) & (token < end), r, jnp.zeros_like(r))
                return jnp.concatenate(gs, axis=1), r

            @pl.when((blocks == n) & (s < 7))
            def _():
                g, r = factors()
                p = jnp.dot(g, r, preferred_element_type=F32)
                acc[...] += p * p

            @pl.when((blocks == n) & (s == 7))
            def _():
                g, r = factors()
                for c, (at, wide) in enumerate(CUTS):
                    cols = pl.ds(at, wide)
                    p = jnp.dot(g, r[:, at : at + wide], preferred_element_type=F32)
                    acc[:, cols] = (acc[:, cols] + p * p) * 0.125
                    results(c).start()

        return end

    lax.fori_loop(0, 8, add, 0)
    for c in range(len(CUTS)):
        results(c).wait()


def fit_call(lengths, r, gt):
    hbm = pl.BlockSpec(memory_space=pl.ANY)
    return pl.pallas_call(
        fit_kernel,
        out_shape=jax.ShapeDtypeStruct((FEAT, COLS), F32),
        in_specs=[pl.BlockSpec(memory_space=pltpu.SMEM), hbm, hbm],
        out_specs=hbm,
        scratch_shapes=[
            pltpu.VMEM((4, 4, 128, COLS), BF), pltpu.VMEM((4, 4, FEAT, 128), BF), pltpu.VMEM((FEAT, COLS), F32),
            pltpu.SemaphoreType.DMA((4, 2)), pltpu.SemaphoreType.DMA((4,)),
        ],
        compiler_params=pltpu.CompilerParams(vmem_limit_bytes=58 * 2**20),
        name="sequence_products",
    )(lengths, r, gt)


def shards(gate_pre, up_pre, out_grad, basis_in, basis_out, lengths):
    r, gt = gather_call(gate_pre, up_pre, out_grad, basis_in, basis_out)
    return fit_call(lengths, r, gt)


def solution(mesh):
    return jax.shard_map(
        shards,
        mesh=mesh,
        in_specs=(
            P(("batch", "grid"), "tensor"),
            P(("batch", "grid"), "tensor"),
            P(("batch", "grid"), "tensor"),
            P("tensor", ("batch", "grid")),
            P("tensor", None),
            P(),
        ),
        out_specs=P("tensor", ("batch", "grid")),
        check_vma=False,
    )
```

```python
import functools

import jax
import jax.numpy as jnp
from jax import lax
from jax.experimental import pallas as pl
from jax.experimental.pallas import tpu as pltpu
from jax.sharding import PartitionSpec as P

MESH = pl.DeviceIdType.MESH
BF = jnp.bfloat16
F32 = jnp.float32

TOK = 128
HALF = 64
QUART = 32
HID = 3456
COLS = 896
FEAT = 640
D = 5120
NT = 8
STEPS = 4
OWN = 8
PER = 6


def gather_kernel(
    gate_hbm, up_hbm, grad_hbm, bin_hbm, bout_hbm, r_hbm, gt_hbm,
    gate_v, up_v, grad_v, bin_v, bout_v,
    abuf, pbuf, crecv, zsend, zrecv, rbuf, gpart, gcrecv, gzrecv, gx, gy,
    load_sem, xy_send, xy_recv, ce_send, ce_recv, rs_send, rs_recv, ag_send, ag_recv, cf_send, cf_recv,
    gr_send, gr_recv, gg_send, gg_recv, out_sem,
):
    xl = lax.axis_index("batch")
    me = lax.axis_index("tensor")
    gi = lax.axis_index("grid")
    x = lax.div(gi, 4) * 2 + xl
    y = lax.rem(gi, 4)
    z = lax.div(me, 2)
    core = lax.rem(me, 2)

    def at(dx, dy):
        xx = lax.rem(x + (dx + 4), 4)
        yy = lax.rem(y + (dy + 4), 4)
        return (lax.rem(xx, 2), me, lax.div(xx, 2) * 4 + yy)

    def block_of(dx, dy):
        b, _, g = at(dx, dy)
        return b * 8 + g

    def zpeer(k):
        return (xl, lax.rem(z + k, 4) * 2 + core, gi)

    partner = (xl, z * 2 + 1 - core, gi)
    xp, xm, yp, ym = at(1, 0), at(-1, 0), at(0, 1), at(0, -1)

    loads = [
        pltpu.make_async_copy(s, d, load_sem.at[i])
        for i, (s, d) in enumerate(
            [(gate_hbm, gate_v), (up_hbm, up_v), (grad_hbm, grad_v), (bout_hbm, bout_v), (bin_hbm, bin_v)]
        )
    ]
    loads[0].start()
    loads[1].start()

    barrier = pltpu.get_barrier_semaphore()
    for dev in [xp, xm, yp, ym, partner, zpeer(1), zpeer(2), zpeer(3)]:
        pl.semaphore_signal(barrier, inc=1, device_id=dev, device_id_type=MESH)
    pl.semaphore_wait(barrier, 8)

    def remote(src, dst, ss, rs, dev):
        return pltpu.make_async_remote_copy(
            src_ref=src, dst_ref=dst, send_sem=ss, recv_sem=rs, device_id=dev, device_id_type=MESH
        )

    def rows_at(i, n):
        return pl.ds(pl.multiple_of(i, 16), n)

    def piece(i, off=0, n=HALF):
        return abuf.at[rows_at(i * HALF + off, n)]

    def xy(step, k, part=0):
        first = isinstance(step, int) and step < 0
        fwd = k % 4 >= 2
        minus = k % 2
        is_y = k >= 4
        if first:
            base = 4 if is_y else 0
            own, near, far = base, base + 1 + minus, base + 3
            dev = ((yp, ym) if is_y else (xp, xm))[minus]
        else:
            b = OWN + PER * step
            own = (4 if is_y else 0) + step
            near = b + (2 if is_y else 0) + minus
            far = b + 4 + (1 if is_y else 0)
            dev = ((xp, xm) if is_y else (yp, ym))[minus]
        if fwd:
            src, dst = piece(near, QUART * minus, QUART), piece(far, QUART * minus, QUART)
        elif first:
            src, dst = piece(own, QUART * part, QUART), piece(near, QUART * part, QUART)
        else:
            src, dst = piece(own), piece(near)
        sem = (k + 40 * part if first else 8 + 8 * step + k)
        return remote(src, dst, xy_send.at[sem], xy_recv.at[sem], dev)

    def swap(gran, row, n):
        h = n // 2
        return remote(
            pbuf.at[rows_at(row + (1 - core) * h, h)], crecv.at[rows_at(lax.div(row, 2), h)],
            ce_send.at[gran], ce_recv.at[gran], partner,
        )

    def rs_copy(gran, row, n, k):
        m = n // 8
        return remote(
            zsend.at[rows_at(lax.div(row, 2) + lax.rem(z + k, 4) * m, m)],
            zrecv.at[k - 1, rows_at(lax.div(row, 8), m)],
            rs_send.at[gran, k - 1], rs_recv.at[gran, k - 1], zpeer(k),
        )

    def ag_copy(gran, row, n, k):
        m = n // 8
        here = rbuf.at[rows_at(row + core * (n // 2) + z * m, m)]
        return remote(here, here, ag_send.at[gran, k - 1], ag_recv.at[gran, k - 1], zpeer(k))

    def ag_arrival(gran, row, n, k):
        m = n // 8
        there = rbuf.at[rows_at(row + core * (n // 2) + lax.rem(z + 4 - k, 4) * m, m)]
        return remote(there, there, ag_send.at[gran, k - 1], ag_recv.at[gran, k - 1], zpeer(k))

    def half_copy(gran, row, n, c):
        there = rbuf.at[rows_at(row + c * (n // 2), n // 2)]
        return remote(there, there, cf_send.at[gran], cf_recv.at[gran], partner)

    def multiply(gran, row, n):
        rows = rows_at(row, n)
        pbuf[rows, :] = jnp.dot(abuf[rows, :], bin_v[...], preferred_element_type=F32)
        swap(gran, row, n).start()

    def pair(gran, row, n):
        h = n // 2
        swap(gran, row, n).wait_recv()
        mine = pbuf[rows_at(row + core * h, h), :]
        theirs = crecv[rows_at(lax.div(row, 2), h), :]
        zsend[rows_at(lax.div(row, 2), h), :] = (mine + theirs).astype(BF)
        for k in (2, 1, 3):
            rs_copy(gran, row, n, k).start()

    def combine(gran, row, n):
        h, m = n // 2, n // 8
        total = pbuf[rows_at(row + core * h + z * m, m), :] + crecv[rows_at(lax.div(row, 2) + z * m, m), :]
        for k in (1, 3, 2):
            rs_copy(gran, row, n, k).wait_recv()
            total = total + zrecv[k - 1, rows_at(lax.div(row, 8), m), :].astype(F32)
        rbuf[rows_at(row + core * h + z * m, m), :] = total.astype(BF)
        for k in (2, 1, 3):
            ag_copy(gran, row, n, k).start()

    def spread(gran, row, n):
        for k in (1, 3, 2):
            ag_arrival(gran, row, n, k).wait_recv()
        half_copy(gran, row, n, core).start()

    def finish(gran, row, n):
        half_copy(gran, row, n, 1 - core).wait_recv()

    def store(i, cx, cy, half):
        return pltpu.make_async_copy(
            rbuf.at[rows_at(i * HALF, HALF)], r_hbm.at[cx, cy, pl.ds(half * HALF, HALF)], out_sem.at[i]
        )

    def store_own():
        return [store(i, i, 0, 0) for i in range(4)] + [store(4 + i, 0, i, 1) for i in range(4)]

    def store_near(j):
        b = OWN + PER * j
        return [store(b, j, 1, 0), store(b + 1, j, 2, 0), store(b + 2, 1, j, 1), store(b + 3, 2, j, 1)]

    def store_far(j):
        b = OWN + PER * j
        return [store(b + 4, j, 3, 0), store(b + 5, 3, j, 1)]

    def store_gradient(i):
        return [
            pltpu.make_async_copy(gx.at[i], gt_hbm.at[:, i, pl.ds(0, GH)], out_sem.at[32 + i]),
            pltpu.make_async_copy(gy.at[i], gt_hbm.at[i, :, pl.ds(GH, GH)], out_sem.at[36 + i]),
        ]

    def start(copies):
        for c in copies:
            c.start()

    def sent(gran, row, n):
        swap(gran, row, n).wait_send()
        half_copy(gran, row, n, core).wait_send()
        for k in (1, 2, 3):
            rs_copy(gran, row, n, k).wait_send()
            ag_copy(gran, row, n, k).wait_send()

    GH = FEAT // 2
    GQ = FEAT // 4

    def gg(phase, k):
        fwd = k % 4 >= 2
        minus = k % 2
        is_y = k >= 4
        buf = gy if is_y else gx
        if phase == 0:
            dev = ((yp, ym) if is_y else (xp, xm))[minus]
            if fwd:
                rows = pl.ds(GQ * minus, GQ)
                src, dst = buf.at[0, 1 + minus, rows], buf.at[0, 3, rows]
            else:
                src, dst = buf.at[0, 0], buf.at[0, 1 + minus]
        else:
            dev = ((xp, xm) if is_y else (yp, ym))[minus]
            if fwd:
                one = 2 * (phase - 1) + minus
                src, dst = buf.at[1 + minus, one], buf.at[3, one]
            else:
                part = pl.ds(2 * (phase - 1), 2)
                src, dst = buf.at[0, part], buf.at[1 + minus, part]
        sem = 8 * phase + k
        return remote(src, dst, gg_send.at[sem], gg_recv.at[sem], dev)

    def gr_swap():
        return remote(gpart.at[1 - core], gcrecv, gr_send.at[0], gr_recv.at[0], partner)

    def gr_copy(k):
        return remote(gpart.at[core, lax.rem(z + k, 4)], gzrecv.at[k - 1], gr_send.at[k], gr_recv.at[k], zpeer(k))

    loads[0].wait()
    loads[1].wait()
    for part in (0, 1):
        for half, i in ((0, 0), (1, 4)):
            rows = pl.ds(half * HALF + part * QUART, QUART)
            g = gate_v[rows, :].astype(F32)
            u = up_v[rows, :].astype(F32)
            abuf[pl.ds(i * HALF + part * QUART, QUART), :] = (g / (1.0 + jnp.exp(-g)) * u).astype(BF)
            for k in (0, 1):
                xy(-1, 4 * half + k, part).start()
            if part == 0 and half == 1:
                for c in loads[2:]:
                    c.start()

    loads[2].wait()
    loads[3].wait()

    def rotate(c, carry):
        cols = pl.ds(pl.multiple_of(c * FEAT, 128), FEAT)
        gpart[lax.rem(c, 2), lax.div(c, 2)] = jnp.dot(grad_v[...], bout_v[:, cols], preferred_element_type=F32)
        return carry

    lax.fori_loop(0, NT, rotate, 0)
    gr_swap().start()
    for k in (0, 1, 4, 5):
        xy(0, k).start()
    gr_swap().wait_recv()
    for k in (2, 1, 3):
        there = lax.rem(z + k, 4)
        gpart[core, there] = gpart[core, there] + gcrecv[there]
        gr_copy(k).start()
    loads[4].wait()

    for k in (0, 1, 4, 5):
        for part in (0, 1):
            xy(-1, k, part).wait_recv()
        xy(-1, k + 2).start()
    for k in (0, 1, 4, 5):
        xy(1, k).start()

    def near_of(j):
        return (2 + 2 * j, OWN * HALF + j * (PER * HALF), 256)

    def far_of(j):
        return (3 + 2 * j, OWN * HALF + j * (PER * HALF) + 256, 128)

    own = ((0, 0, 256), (1, 256, 256))

    def pass_on(j):
        for k in (0, 1, 4, 5):
            xy(j, k).wait_recv()
            xy(j, k + 2).start()

        @pl.when(j < 2)
        def _():
            for k in (0, 1, 4, 5):
                xy(j + 2, k).start()

        @pl.when(j == 2)
        def _():
            for k in (0, 1, 4, 5):
                gg(0, k).start()

        @pl.when(j == 3)
        def _():
            for k in (0, 1, 4, 5):
                gg(0, k).wait_recv()
                gg(0, k + 2).start()
                gg(1, k).start()

    def step(j, carry):
        pass_on(j)

        multiply(*near_of(j))

        @pl.when(j == 1)
        def _():
            for g in own:
                combine(*g)

        @pl.when(j > 1)
        def _():
            combine(*far_of(j - 2))

        @pl.when(j > 0)
        def _():
            spread(*near_of(j - 1))

        pair(*near_of(j))

        @pl.when(j == 0)
        def _():
            for k in (2, 3, 6, 7):
                xy(-1, k).wait_recv()
            lax.fori_loop(0, 2, lambda g, c: (multiply(g, g * 256, 256), c)[1], 0)
            for g in own:
                pair(*g)

        @pl.when(j > 0)
        def _():
            for k in (2, 3, 6, 7):
                xy(j - 1, k).wait_recv()
            multiply(*far_of(j - 1))
            pair(*far_of(j - 1))

        combine(*near_of(j))

        @pl.when(j == 0)
        def _():
            share = gpart[core, z] + gcrecv[z]
            for k in (1, 3, 2):
                gr_copy(k).wait_recv()
                share = share + gzrecv[k - 1]
            share = share.T.astype(BF)
            gx[0, 0] = share[:GH]
            gy[0, 0] = share[GH:]

        @pl.when(j == 1)
        def _():
            for g in own:
                spread(*g)
            for k in range(8):
                xy(-1, k).wait_send()
            for k in (0, 1, 4, 5):
                xy(-1, k, 1).wait_send()
            gr_swap().wait_send()
            for k in (1, 2, 3):
                gr_copy(k).wait_send()

        @pl.when(j > 1)
        def _():
            spread(*far_of(j - 2))
            for k in range(8):
                xy(j - 2, k).wait_send()

        @pl.when(j == 2)
        def _():
            for g in own:
                finish(*g)
                sent(*g)
            start(store_own())

        @pl.when(j == 3)
        def _():
            for g in (near_of(0), far_of(0)):
                finish(*g)
                sent(*g)
            start(store_near(0) + store_far(0))

        return carry

    lax.fori_loop(0, STEPS, step, 0)

    def forward(phase):
        for k in (0, 1, 4, 5):
            gg(phase, k).wait_recv()
            gg(phase, k + 2).start()

    for k in (2, 3, 6, 7):
        xy(3, k).wait_recv()
    multiply(*far_of(3))
    for k in (2, 3, 6, 7):
        gg(0, k).wait_recv()
    for k in (0, 1, 4, 5):
        gg(2, k).start()
    pair(*far_of(3))
    combine(*far_of(2))
    forward(1)
    spread(*near_of(3))
    combine(*far_of(3))
    forward(2)
    spread(*far_of(2))
    start(store_gradient(1) + store_gradient(2))
    for g in (far_of(2), near_of(3)):
        finish(*g)
    start(store_far(2) + store_near(3))
    for g in (near_of(1), near_of(2)):
        finish(*g)
    start(store_near(1) + store_near(2))
    spread(*far_of(3))
    finish(*far_of(1))
    start(store_far(1) + store_gradient(0))
    for g in (near_of(1), far_of(1), near_of(2), far_of(2), near_of(3)):
        sent(*g)
    for j in (2, 3):
        for k in range(8):
            xy(j, k).wait_send()
    for k in range(8):
        gg(0, k).wait_send()
    early = store_own() + store_near(3)
    for j in range(3):
        early += store_near(j) + store_far(j) + store_gradient(j)
    for c in early:
        c.wait()
    for phase in (1, 2):
        for k in (2, 3, 6, 7):
            gg(phase, k).wait_recv()
    start(store_gradient(3))
    finish(*far_of(3))
    start(store_far(3))
    for phase in (1, 2):
        for k in range(8):
            gg(phase, k).wait_send()
    sent(*far_of(3))
    for c in store_gradient(3) + store_far(3):
        c.wait()


def gather_call(gate, up, grad, basis_in, basis_out):
    vm = pltpu.VMEM
    dma = pltpu.SemaphoreType.DMA
    hbm = pl.BlockSpec(memory_space=pl.ANY)
    return pl.pallas_call(
        gather_kernel,
        out_shape=(
            jax.ShapeDtypeStruct((4, 4, TOK, COLS), BF),
            jax.ShapeDtypeStruct((4, 4, FEAT, TOK), BF),
        ),
        in_specs=[hbm] * 5,
        out_specs=(hbm, hbm),
        scratch_shapes=[
            vm((TOK, HID), BF), vm((TOK, HID), BF), vm((TOK, FEAT), BF), vm((HID, COLS), BF), vm((FEAT, D), BF),
            vm((2048, HID), BF), vm((2048, COLS), F32), vm((1024, COLS), F32), vm((1024, COLS), BF),
            vm((3, 256, COLS), BF), vm((2048, COLS), BF),
            vm((2, 4, TOK, FEAT), F32), vm((4, TOK, FEAT), F32), vm((3, TOK, FEAT), F32),
            vm((4, 4, FEAT // 2, TOK), BF), vm((4, 4, FEAT // 2, TOK), BF),
            dma((5,)), dma((48,)), dma((48,)), dma((10,)), dma((10,)), dma((10, 3)), dma((10, 3)),
            dma((10, 3)), dma((10, 3)), dma((10,)), dma((10,)),
            dma((4,)), dma((4,)), dma((24,)), dma((24,)), dma((40,)),
        ],
        compiler_params=pltpu.CompilerParams(
            collective_id=0, has_side_effects=True, vmem_limit_bytes=58 * 2**20
        ),
        name="rotate_gather",
    )(gate, up, grad, basis_in, basis_out)


KB = 128
CUTS = ((0, 256), (256, 256), (512, 256), (768, 128))


def fit_kernel(lengths, r_hbm, gt_hbm, out_hbm, r_ref, g_ref, acc, in_sem, out_sem):
    gi = lax.axis_index("grid")
    x = lax.div(gi, 4) * 2 + lax.axis_index("batch")
    y = lax.rem(gi, 4)

    def code(there, here):
        d = lax.rem(there - here + 4, 4)
        return jnp.where(d == 0, 0, jnp.where(d == 3, 1, d + 1))

    def load(quarter):
        cx = code(lax.rem(quarter, 2) * 2 + lax.div(quarter, 2), x)
        return (
            pltpu.make_async_copy(r_hbm.at[cx], r_ref.at[quarter], in_sem.at[quarter, 0]),
            pltpu.make_async_copy(gt_hbm.at[cx], g_ref.at[quarter], in_sem.at[quarter, 1]),
        )

    for quarter in range(4):
        for c in load(quarter):
            c.start()
    acc[...] = jnp.zeros_like(acc)

    def results(c):
        cols = pl.ds(*CUTS[c])
        return pltpu.make_async_copy(acc.at[:, cols], out_hbm.at[:, cols], out_sem.at[c])

    def add(s, begin):
        end = begin + lengths[s]
        first = lax.div(begin, KB)
        blocks = lax.div(end + KB - 1, KB) - first

        @pl.when(s < 4)
        def _():
            for c in load(s):
                c.wait()

        for n in range(1, 2 + 512 // KB):

            def factors():
                rs, gs = [], []
                for i in range(n * KB // 128):
                    block = first * (KB // 128) + i
                    quarter, cy = lax.div(block, 4), code(lax.rem(block, 4), y)
                    rs.append(r_ref[quarter, cy])
                    gs.append(g_ref[quarter, cy])
                r = jnp.concatenate(rs, axis=0)
                token = first * KB + lax.broadcasted_iota(jnp.int32, r.shape, 0)
                r = jnp.where((token >= begin) & (token < end), r, jnp.zeros_like(r))
                return jnp.concatenate(gs, axis=1), r

            @pl.when((blocks == n) & (s < 7))
            def _():
                g, r = factors()
                p = jnp.dot(g, r, preferred_element_type=F32)
                acc[...] += p * p

            @pl.when((blocks == n) & (s == 7))
            def _():
                g, r = factors()
                for c, (at, wide) in enumerate(CUTS):
                    cols = pl.ds(at, wide)
                    p = jnp.dot(g, r[:, at : at + wide], preferred_element_type=F32)
                    acc[:, cols] = (acc[:, cols] + p * p) * 0.125
                    results(c).start()

        return end

    lax.fori_loop(0, 8, add, 0)
    for c in range(len(CUTS)):
        results(c).wait()


def fit_call(lengths, r, gt):
    hbm = pl.BlockSpec(memory_space=pl.ANY)
    return pl.pallas_call(
        fit_kernel,
        out_shape=jax.ShapeDtypeStruct((FEAT, COLS), F32),
        in_specs=[pl.BlockSpec(memory_space=pltpu.SMEM), hbm, hbm],
        out_specs=hbm,
        scratch_shapes=[
            pltpu.VMEM((4, 4, 128, COLS), BF), pltpu.VMEM((4, 4, FEAT, 128), BF), pltpu.VMEM((FEAT, COLS), F32),
            pltpu.SemaphoreType.DMA((4, 2)), pltpu.SemaphoreType.DMA((4,)),
        ],
        compiler_params=pltpu.CompilerParams(vmem_limit_bytes=58 * 2**20),
        name="sequence_products",
    )(lengths, r, gt)


def shards(gate_pre, up_pre, out_grad, basis_in, basis_out, lengths):
    r, gt = gather_call(gate_pre, up_pre, out_grad, basis_in, basis_out)
    return fit_call(lengths, r, gt)


def solution(mesh):
    return jax.shard_map(
        shards,
        mesh=mesh,
        in_specs=(
            P(("batch", "grid"), "tensor"),
            P(("batch", "grid"), "tensor"),
            P(("batch", "grid"), "tensor"),
            P("tensor", ("batch", "grid")),
            P("tensor", None),
            P(),
        ),
        out_specs=P("tensor", ("batch", "grid")),
        check_vma=False,
    )
```
